128 devices in a mesh: dp: 8 (over z, core), expert: 16 (over y, x).
Axes of the slice: x: 4, y: 4, z: 4, core: 2. Of those that a mesh axis runs over, the one named last changes fastest.
Arguments:
- tokens: bfloat16 [16384, 2048], P(('dp', 'expert')), may hold values from -6 to 6
- expert_ids: int32 [16384, 8], P(('dp', 'expert')), may hold values from 0 to 127, as said below
- gate_codes: int32 [16384, 8], P(('dp', 'expert')), may hold values from 1 to 255
- grad_out: bfloat16 [16384, 2048], P(('dp', 'expert')), may hold values from -6 to 6
- w_gate: bfloat16 [128, 2048, 768], P('expert', 'dp'), may hold values from -0.125 to 0.125
- w_up: bfloat16 [128, 2048, 768], P('expert', 'dp'), may hold values from -0.125 to 0.125
- w_down: bfloat16 [128, 2048, 768], P('expert', 'dp'), may hold values from -0.21875 to 0.21875
Outputs:
- mixed: bfloat16 [16384, 2048], P(('dp', 'expert'))
- tokens_grad: bfloat16 [16384, 2048], P(('dp', 'expert'))
- w_gate_grad: bfloat16 [128, 2048, 768], P('expert', 'dp')
- w_up_grad: bfloat16 [128, 2048, 768], P('expert', 'dp')
- w_down_grad: bfloat16 [128, 2048, 768], P('expert', 'dp')
The draws below stay inside these ranges and needn't reach their ends.
Inputs may be any that keep to these rules, and one draw needn't show every extreme that they name: `expert_ids`: each row names 8 different experts. Among the routes of the 128 tokens of one device (aligned blocks of rows), no expert is named more than 16 times, and some expert is named exactly 16 times by the tokens of every device.
All inputs are finite; a program needn't handle non-finite values.
Results may differ from the reference program's by a relative error of at most 0.0064.
Values may be sent and summed in bfloat16 or wider, within the bound.
A program may use at most 256 MiB of HBM per device.

```python
import jax
import jax.numpy as jnp
from jax import lax

D = 2048
FF = 768
TOP = 8
TOK_DEV = 128
EXPERTS = 128
CAP = 16
TOKENS = 16384
N_DP = 8
N_EXPERT = 16


def route_block(subkey, hot_expert, popularity):
    need_count = TOK_DEV * TOP
    copies = EXPERTS * CAP
    noise_add = jax.random.randint(jax.random.fold_in(subkey, 1), (EXPERTS, CAP), 0, 24)
    scores = popularity[:, None] - 16 * jnp.arange(CAP, dtype=jnp.int32)[None, :] + noise_add
    scores = jnp.where(jnp.arange(EXPERTS, dtype=jnp.int32)[:, None] == hot_expert, 1 << 20, scores).reshape(-1)
    shuffle = jax.random.permutation(jax.random.fold_in(subkey, 2), copies)
    ranked = jnp.argsort(-scores[shuffle], stable=True)
    chosen = shuffle[ranked[:need_count]]
    counts = jnp.zeros((EXPERTS,), jnp.int32).at[chosen // CAP].add(1)
    bounds = jnp.cumsum(counts)
    sorted_ids = jnp.searchsorted(bounds, jnp.arange(need_count, dtype=jnp.int32), side='right').astype(jnp.int32)
    layout = sorted_ids.reshape(TOP, TOK_DEV).T
    token_perm = jax.random.permutation(jax.random.fold_in(subkey, 3), TOK_DEV)
    route_perm = jax.random.permutation(jax.random.fold_in(subkey, 4), TOP)
    return layout[token_perm][:, route_perm]


def draw_expert_ids(key, part):
    key = jax.random.fold_in(key, 7)
    hot_expert = jax.random.randint(jax.random.fold_in(key, 1), (), 0, EXPERTS)
    popularity = jax.random.randint(jax.random.fold_in(key, 2), (EXPERTS,), 0, 32 * CAP)
    blocks = TOKENS // TOK_DEV
    key_list = jax.vmap(lambda number: jax.random.fold_in(key, number + 100))(jnp.arange(blocks))
    routed = jax.vmap(lambda subkey: route_block(subkey, hot_expert, popularity))(key_list)
    return routed.reshape(TOKENS, TOP).astype(jnp.int32)


def with_ends(drawn, stream_key, low, high):
    longest = drawn.shape.index(max(drawn.shape))
    spots = []
    for shift in (0, 1):
        where = [jax.random.randint(jax.random.fold_in(stream_key, axis), (), 0, length) for axis, length in enumerate(drawn.shape)]
        where[longest] = (where[longest] + shift) % drawn.shape[longest]
        spots.append(tuple(where))
    return drawn.at[spots[0]].set(low).at[spots[1]].set(high)


def steps_of(own_key, shape, pieces, low, top_value):
    gain, own = 1.0, jax.random.fold_in(own_key, 6)
    for dim, shards_of in pieces:
        draws = jnp.exp(jax.random.uniform(jax.random.fold_in(own, dim), (shards_of,), jnp.float32, low / len(pieces), top_value / len(pieces)))
        gain = gain * jnp.repeat(draws, shape[dim] // shards_of).reshape([-1 if axis == dim else 1 for axis in range(len(shape))])
    return gain


def gaussian(stream_key, dims, deviation, reach, split=(), kind=jnp.bfloat16):
    values = jax.random.normal(stream_key, dims, jnp.float32) * deviation
    if len(split) > 0:
        values = steps_of(stream_key, dims, split, -0.22, 0.18) * values
    return jnp.clip(values, min=-reach, max=reach).astype(kind)


def setup_inputs(seed: int = 0) -> dict:
    splits = jax.random.split(jax.random.key(seed), 8)
    return {
        "tokens": gaussian(splits[0], (TOKENS, D), 1.0, 6.0, ((0, 128),)),
        "expert_ids": draw_expert_ids(jax.random.fold_in(splits[7], 71), 0),
        "gate_codes": with_ends(jax.random.randint(splits[2], (TOKENS, TOP), 1, 256), jax.random.fold_in(splits[2], 1), 1, 255).astype(jnp.int32),
        "grad_out": gaussian(splits[3], (TOKENS, D), 1.0, 6.0, ((0, 128),)),
        "w_gate": gaussian(splits[4], (EXPERTS, D, FF), D ** -0.5, 0.125, ((0, 16), (1, 8))),
        "w_up": gaussian(splits[5], (EXPERTS, D, FF), D ** -0.5, 0.125, ((0, 16), (1, 8))),
        "w_down": gaussian(splits[6], (EXPERTS, D, FF), FF ** -0.5, 0.21875, ((0, 16), (1, 8))),
    }


def expert_forward(row_set, gate_weight, up_weight, down_weight):
    gate_pre = jnp.dot(row_set, gate_weight, preferred_element_type=jnp.float32)
    up_pre = jnp.dot(row_set, up_weight, preferred_element_type=jnp.float32)
    hidden = (gate_pre * jax.nn.sigmoid(gate_pre) * up_pre).astype(jnp.bfloat16)
    output = lax.dot_general(hidden, down_weight, (((1,), (1,)), ((), ())), preferred_element_type=jnp.float32)
    return output.astype(jnp.bfloat16), gate_pre, up_pre, hidden


def expert_backward(row_set, gate_pre, up_pre, hidden, upstream, gate_weight, up_weight, down_weight):
    hidden_grad = jnp.dot(upstream, down_weight, preferred_element_type=jnp.float32)
    sigmoid = jax.nn.sigmoid(gate_pre)
    gate_grad = (hidden_grad * up_pre * sigmoid * (1.0 + gate_pre * (1.0 - sigmoid))).astype(jnp.bfloat16)
    up_grad = (hidden_grad * gate_pre * sigmoid).astype(jnp.bfloat16)
    contract = (((1,), (1,)), ((), ()))
    route_grad = lax.dot_general(gate_grad, gate_weight, contract, preferred_element_type=jnp.float32)
    route_grad = route_grad + lax.dot_general(up_grad, up_weight, contract, preferred_element_type=jnp.float32)
    across = (((0,), (0,)), ((), ()))
    gate_total = lax.dot_general(row_set, gate_grad, across, preferred_element_type=jnp.float32)
    up_total = lax.dot_general(row_set, up_grad, across, preferred_element_type=jnp.float32)
    down_total = lax.dot_general(upstream, hidden, across, preferred_element_type=jnp.float32)
    return route_grad.astype(jnp.bfloat16), gate_total, up_total, down_total


def reference(tokens, expert_ids, gate_codes, grad_out, w_gate, w_up, w_down):
    pair_count = TOKENS * TOP
    most_rows = N_DP * N_EXPERT * CAP
    flat_ids = expert_ids.reshape(-1)
    gate_values = jnp.concatenate([gate_codes.reshape(-1).astype(jnp.float32) / 256.0, jnp.zeros((1,), jnp.float32)])
    zero_row = jnp.zeros((1, D), tokens.dtype)
    padded_tokens = jnp.concatenate([tokens, zero_row])
    padded_grad = jnp.concatenate([grad_out, zero_row])

    def one_expert(carried, expert_index):
        mixed_acc, grad_acc = carried
        picked = jnp.nonzero(flat_ids == expert_index, size=most_rows, fill_value=pair_count)[0].astype(jnp.int32)
        owner_row = jnp.where(picked < pair_count, picked // TOP, TOKENS).astype(jnp.int32)
        row_set = padded_tokens[owner_row]
        weights_now = gate_values[picked][:, None]
        upstream = (weights_now * padded_grad[owner_row].astype(jnp.float32)).astype(jnp.bfloat16)
        output, gate_pre, up_pre, hidden = expert_forward(row_set, w_gate[expert_index], w_up[expert_index], w_down[expert_index])
        route_grad, gate_total, up_total, down_total = expert_backward(row_set, gate_pre, up_pre, hidden, upstream, w_gate[expert_index], w_up[expert_index], w_down[expert_index])
        mixed_acc = mixed_acc.at[owner_row].add(weights_now * output.astype(jnp.float32))
        grad_acc = grad_acc.at[owner_row].add(route_grad.astype(jnp.float32))
        return (mixed_acc, grad_acc), (gate_total.astype(jnp.bfloat16), up_total.astype(jnp.bfloat16), down_total.astype(jnp.bfloat16))

    initial = (jnp.zeros((TOKENS + 1, D), jnp.float32), jnp.zeros((TOKENS + 1, D), jnp.float32))
    finals, grads = lax.scan(one_expert, initial, jnp.arange(EXPERTS, dtype=jnp.int32))
    mixed = finals[0][:TOKENS].astype(jnp.bfloat16)
    tokens_grad = finals[1][:TOKENS].astype(jnp.bfloat16)
    return (mixed, tokens_grad, grads[0], grads[1], grads[2])
```

```python
import functools

import jax
import jax.numpy as jnp
from jax import lax
from jax.experimental import pallas as pl
from jax.experimental.pallas import tpu as pltpu
from jax.sharding import PartitionSpec as P

BF16 = jnp.bfloat16
F32 = jnp.float32
MESH = pl.DeviceIdType.MESH
ANY = pl.BlockSpec(memory_space=pl.ANY)
DP = 8
EP = 16
SIDE = 4
CAP = 16
TOK = 128


def column_peer(step):
    me = lax.axis_index("dp")
    z, core = me // 2, me % 2
    dz, flip = step // 2, step % 2
    other = core if flip == 0 else 1 - core
    return ((z + dz) % SIDE) * 2 + other, ((z + SIDE - dz) % SIDE) * 2 + other


def plane_peer(step):
    me = lax.axis_index("expert")
    y, x = me // SIDE, me % SIDE
    dy, dx = step // SIDE, step % SIDE
    ahead = ((y + dy) % SIDE) * SIDE + (x + dx) % SIDE
    behind = ((y + SIDE - dy) % SIDE) * SIDE + (x + SIDE - dx) % SIDE
    return ahead, behind


PLANE_STEPS = (10, 9, 11, 6, 14, 2, 8, 5, 7, 13, 15, 1, 3, 4, 12)
COLUMN_STEPS = (4, 5, 2, 3, 6, 7, 1)


def greet(column, plane):
    barrier = pltpu.get_barrier_semaphore()
    dp, ep = lax.axis_index("dp"), lax.axis_index("expert")
    count = 0
    for step in column:
        pl.semaphore_signal(barrier, inc=1, device_id=(column_peer(step)[0], ep), device_id_type=MESH)
        count += 1
    for step in plane:
        pl.semaphore_signal(barrier, inc=1, device_id=(dp, plane_peer(step)[0]), device_id_type=MESH)
        count += 1
    pl.semaphore_wait(barrier, count)


def to_column(step, src, dst, send, recv):
    return pltpu.make_async_remote_copy(
        src_ref=src, dst_ref=dst, send_sem=send, recv_sem=recv,
        device_id=(column_peer(step)[0], lax.axis_index("expert")), device_id_type=MESH,
    )


def to_plane(step, src, dst, send, recv):
    return pltpu.make_async_remote_copy(
        src_ref=src, dst_ref=dst, send_sem=send, recv_sem=recv,
        device_id=(lax.axis_index("dp"), plane_peer(step)[0]), device_id_type=MESH,
    )


def gather_kernel(tok, grd, meta, tok_all, grd_all, meta_all, send, recv, fsend, frecv, local):
    me = lax.axis_index("dp")
    greet((2, 4, 6, 1), ())
    pairs = ((meta, meta_all), (tok, tok_all), (grd, grd_all))
    copies = []
    for i, (src, dst) in enumerate(pairs):
        for n, step in enumerate((4, 2, 6, 1)):
            copy = to_column(step, src, dst.at[me], send.at[i, n], recv.at[i, n])
            copy.start()
            copies.append(copy)
    locals_ = []
    for i, (src, dst) in enumerate(pairs):
        copy = pltpu.make_async_copy(src, dst.at[me], local.at[i])
        copy.start()
        locals_.append(copy)
    forwards = []
    for i, (src, dst) in enumerate(pairs):
        for n, step in ((1, 2), (2, 6), (0, 4)):
            behind = column_peer(step)[1]
            copies[4 * i + n].wait_recv()
            copy = to_column(1, dst.at[behind], dst.at[behind], fsend.at[i, n], frecv.at[i, n])
            copy.start()
            forwards.append(copy)
    for i in range(3):
        copies[4 * i + 3].wait_recv()
    for copy in copies:
        copy.wait_send()
    for copy in forwards:
        copy.wait()
    for copy in locals_:
        copy.wait()


def gather_column(tok, grd, meta):
    return pl.pallas_call(
        gather_kernel,
        out_shape=[
            jax.ShapeDtypeStruct((DP,) + tok.shape, tok.dtype),
            jax.ShapeDtypeStruct((DP,) + grd.shape, grd.dtype),
            jax.ShapeDtypeStruct((DP,) + meta.shape, meta.dtype),
        ],
        in_specs=[ANY] * 3,
        out_specs=[ANY] * 3,
        scratch_shapes=[
            pltpu.SemaphoreType.DMA((3, 4)),
            pltpu.SemaphoreType.DMA((3, 4)),
            pltpu.SemaphoreType.DMA((3, 3)),
            pltpu.SemaphoreType.DMA((3, 3)),
            pltpu.SemaphoreType.DMA((3,)),
        ],
        compiler_params=pltpu.CompilerParams(collective_id=0, has_side_effects=True),
        name="gather_column",
    )(tok, grd, meta)


def exchange_kernel(outward, a, b, p, q, r, a_out, b_out, p_out, q_out, r_out,
                    psend, precv, csend, crecv, local):
    dp, ep = lax.axis_index("dp"), lax.axis_index("expert")
    greet(COLUMN_STEPS, PLANE_STEPS)

    def plane_ends(src, dst, target, mine):
        if outward:
            return src.at[:, target], dst.at[mine]
        return src.at[target], dst.at[:, mine]

    copies = []
    for n, step in enumerate(COLUMN_STEPS):
        target = column_peer(step)[0]
        for i, (src, dst) in enumerate(((p, p_out), (q, q_out), (r, r_out))):
            copies.append(to_column(step, src.at[target], dst.at[dp], csend.at[i, n], crecv.at[i, n]))
    for i, (src, dst) in enumerate(((a, a_out), (b, b_out))):
        for n, step in enumerate(PLANE_STEPS):
            target = plane_peer(step)[0]
            ends = plane_ends(src, dst, target, ep)
            copies.append(to_plane(step, *ends, psend.at[i, n], precv.at[i, n]))
    for i, (src, dst) in enumerate(((p, p_out), (q, q_out), (r, r_out))):
        copies.append(pltpu.make_async_copy(src.at[dp], dst.at[dp], local.at[i]))
    for i, (src, dst) in enumerate(((a, a_out), (b, b_out))):
        copies.append(pltpu.make_async_copy(*plane_ends(src, dst, ep, ep), local.at[3 + i]))
    for copy in copies:
        copy.start()
    for copy in copies:
        copy.wait()


def exchange(outward, number, a, b, p, q, r):
    width = a.shape[-1]
    rows = (EP, DP, CAP, width) if outward else (DP, EP, CAP, width)
    return pl.pallas_call(
        functools.partial(exchange_kernel, outward),
        out_shape=[jax.ShapeDtypeStruct(rows, BF16)] * 2 + [jax.ShapeDtypeStruct(p.shape, BF16)] * 3,
        in_specs=[ANY] * 5,
        out_specs=[ANY] * 5,
        scratch_shapes=[
            pltpu.SemaphoreType.DMA((2, EP - 1)),
            pltpu.SemaphoreType.DMA((2, EP - 1)),
            pltpu.SemaphoreType.DMA((3, DP - 1)),
            pltpu.SemaphoreType.DMA((3, DP - 1)),
            pltpu.SemaphoreType.DMA((5,)),
        ],
        compiler_params=pltpu.CompilerParams(collective_id=number, has_side_effects=True),
        name=f"exchange_{number}",
    )(a, b, p, q, r)


def scatter_kernel(a, b, a_out, b_out, own, other, summed, xsend, xrecv, zsend, zrecv, local):
    me = lax.axis_index("dp")
    z, core = me // 2, me % 2
    greet((2, 4, 6, 1), ())
    pairs = ((a, a_out), (b, b_out))
    first, kept = [], []
    for i, (src, _) in enumerate(pairs):
        copy = to_column(1, src.at[:, 1 - core], other.at[i], xsend.at[i], xrecv.at[i])
        copy.start()
        first.append(copy)
        copy = pltpu.make_async_copy(src.at[:, core], own.at[i], local.at[i])
        copy.start()
        kept.append(copy)
    last = []
    for i, (_, dst) in enumerate(pairs):
        first[i].wait_recv()
        kept[i].wait()
        for part in range(SIDE):
            summed[i, part] = (own[i, part].astype(F32) + other[i, part].astype(F32)).astype(BF16)
        for n, step in enumerate((4, 2, 6)):
            copy = to_column(step, summed.at[i, (z + step // 2) % SIDE], dst.at[n], zsend.at[i, n], zrecv.at[i, n])
            copy.start()
            last.append(copy)
        copy = pltpu.make_async_copy(summed.at[i, z], dst.at[3], local.at[2 + i])
        copy.start()
        last.append(copy)
    for copy in last:
        copy.wait()
    for copy in first:
        copy.wait_send()


def scatter_column(a, b):
    _, tok, width = a.shape
    a, b = (v.reshape(SIDE, 2, tok, width) for v in (a, b))
    return pl.pallas_call(
        scatter_kernel,
        out_shape=[jax.ShapeDtypeStruct((SIDE, tok, width), BF16)] * 2,
        in_specs=[ANY] * 2,
        out_specs=[ANY] * 2,
        scratch_shapes=[pltpu.VMEM((2, SIDE, tok, width), BF16)] * 3
        + [
            pltpu.SemaphoreType.DMA((2,)),
            pltpu.SemaphoreType.DMA((2,)),
            pltpu.SemaphoreType.DMA((2, 3)),
            pltpu.SemaphoreType.DMA((2, 3)),
            pltpu.SemaphoreType.DMA((4,)),
        ],
        compiler_params=pltpu.CompilerParams(
            collective_id=3, has_side_effects=True, vmem_limit_bytes=40 * 2**20
        ),
        name="scatter_column",
    )(a, b)


NT = (((1,), (1,)), ((), ()))
TN = (((0,), (0,)), ((), ()))


def dot(a, b, dims=(((1,), (0,)), ((), ()))):
    return lax.dot_general(a, b, dims, preferred_element_type=F32)


def rows_kernel(x, u, wg, wu, wd, out, rg, hid, gg, ug):
    gate, up = dot(x[...], wg[...]), dot(x[...], wu[...])
    s = jax.nn.sigmoid(gate)
    hidden = (gate * s * up).astype(BF16)
    hid[...] = hidden
    out[...] = dot(hidden, wd[...], NT).astype(BF16)
    hg = dot(u[...], wd[...])
    gate_grad = (hg * up * s * (1.0 + gate * (1.0 - s))).astype(BF16)
    up_grad = (hg * gate * s).astype(BF16)
    gg[...] = gate_grad
    ug[...] = up_grad
    rg[...] = (dot(gate_grad, wg[...], NT) + dot(up_grad, wu[...], NT)).astype(BF16)


def expert_rows(x, u, wg, wu, wd):
    rows, width = x.shape
    ff = wg.shape[1]
    block = 256
    wide = pl.BlockSpec((block, width), lambda i: (i, 0))
    thin = pl.BlockSpec((block, ff), lambda i: (i, 0))
    weight = pl.BlockSpec((width, ff), lambda i: (0, 0), pipeline_mode=pl.Buffered(1))
    return pl.pallas_call(
        rows_kernel,
        grid=(rows // block,),
        out_shape=[jax.ShapeDtypeStruct((rows, width), BF16)] * 2
        + [jax.ShapeDtypeStruct((rows, ff), BF16)] * 3,
        in_specs=[wide, wide, weight, weight, weight],
        out_specs=[wide, wide, thin, thin, thin],
        compiler_params=pltpu.CompilerParams(vmem_limit_bytes=56 * 2**20),
        name="expert_rows",
    )(x, u, wg, wu, wd)


def weights_kernel(x, u, hid, gg, ug, dg, du, dd):
    dg[...] = dot(x[...], gg[...], TN).astype(BF16)
    du[...] = dot(x[...], ug[...], TN).astype(BF16)
    dd[...] = dot(u[...], hid[...], TN).astype(BF16)


def expert_weights(x, u, hid, gg, ug):
    rows, width = x.shape
    ff = hid.shape[1]
    block = 256
    slab = pl.BlockSpec((rows, block), lambda i: (0, i))
    whole = pl.BlockSpec((rows, ff), lambda i: (0, 0), pipeline_mode=pl.Buffered(1))
    result = pl.BlockSpec((block, ff), lambda i: (i, 0))
    return pl.pallas_call(
        weights_kernel,
        grid=(width // block,),
        out_shape=[jax.ShapeDtypeStruct((width, ff), BF16)] * 3,
        in_specs=[slab, slab, whole, whole, whole],
        out_specs=[result] * 3,
        compiler_params=pltpu.CompilerParams(vmem_limit_bytes=56 * 2**20),
        name="expert_weights",
    )(x, u, hid, gg, ug)


def local(tokens, expert_ids, gate_codes, grad_out, w_gate, w_up, w_down):
    dp = lax.axis_index("dp")
    tok, width = tokens.shape
    ff = w_gate.shape[-1]
    meta = (expert_ids * 256 + gate_codes).T
    tok_all, grd_all, meta_all = gather_column(tokens, grad_out, meta)
    ids, codes = meta_all // 256, meta_all % 256
    mine = jnp.arange(EP, dtype=jnp.int32) * DP + dp
    named = ids[:, None] == mine[None, :, None, None]
    has = jnp.any(named, axis=2)
    gate = jnp.sum(jnp.where(named, codes[:, None], 0), axis=2).astype(F32) / 256.0
    earlier = jnp.triu(jnp.ones((tok, tok), BF16), 1)
    rank = jnp.dot(has.astype(BF16), earlier, preferred_element_type=F32).astype(jnp.int32)
    slot = jnp.where(has, rank, -1)[:, :, None, :]
    pick = slot == jnp.arange(CAP, dtype=jnp.int32)[None, None, :, None]
    weight = jnp.where(pick, gate[:, :, None, :], 0.0).astype(BF16).reshape(DP, EP * CAP, tok)
    pick = pick.astype(BF16).reshape(DP, EP * CAP, tok)
    gathers = (((2,), (1,)), ((0,), (0,)))
    sends = (((1,), (1,)), ((0,), (0,)))

    def spread(matrix, rows):
        picked = lax.dot_general(matrix, rows, gathers, preferred_element_type=F32)
        return picked.astype(BF16).reshape(DP, EP, CAP, width)

    def collect(matrix, rows):
        summed = lax.dot_general(
            matrix, rows.reshape(DP, EP * CAP, width), sends, preferred_element_type=F32
        )
        return summed.astype(BF16)

    x, u, wg, wu, wd = exchange(
        True, 1, spread(pick, tok_all), spread(weight, grd_all), w_gate, w_up, w_down
    )
    x, u = x.reshape(-1, width), u.reshape(-1, width)
    wg, wu, wd = (w.reshape(width, ff) for w in (wg, wu, wd))
    out, rg, hid, gg, ug = expert_rows(x, u, wg, wu, wd)
    grads = expert_weights(x, u, hid, gg, ug)
    shape = (EP, DP, CAP, width)
    out, rg, dg, du, dd = exchange(
        False, 2, out.reshape(shape), rg.reshape(shape), *(g.reshape(DP, -1, ff) for g in grads)
    )
    mixed, tokens_grad = scatter_column(collect(weight, out), collect(pick, rg))
    mixed, tokens_grad = (
        jnp.sum(v.astype(F32), axis=0).astype(BF16) for v in (mixed, tokens_grad)
    )
    return mixed, tokens_grad, dg, du, dd


def solution(mesh):
    rows, weights = P(("dp", "expert"), None), P("expert", "dp", None)
    return jax.shard_map(
        local,
        mesh=mesh,
        in_specs=(rows,) * 4 + (weights,) * 3,
        out_specs=(rows,) * 2 + (weights,) * 3,
        check_vma=False,
    )
```

```python
import jax
import jax.numpy as jnp
from jax import lax
from jax.experimental import pallas as pl
from jax.experimental.pallas import tpu as pltpu
from jax.sharding import PartitionSpec as P

BF16 = jnp.bfloat16
F32 = jnp.float32
MESH = pl.DeviceIdType.MESH
ANY = pl.BlockSpec(memory_space=pl.ANY)
DP = 8
EP = 16
SIDE = 4
CAP = 16
TOK = 128


def column_peer(step):
    me = lax.axis_index("dp")
    z, core = me // 2, me % 2
    dz, flip = step // 2, step % 2
    other = core if flip == 0 else 1 - core
    return ((z + dz) % SIDE) * 2 + other, ((z + SIDE - dz) % SIDE) * 2 + other


def plane_peer(step):
    me = lax.axis_index("expert")
    y, x = me // SIDE, me % SIDE
    dy, dx = step // SIDE, step % SIDE
    ahead = ((y + dy) % SIDE) * SIDE + (x + dx) % SIDE
    behind = ((y + SIDE - dy) % SIDE) * SIDE + (x + SIDE - dx) % SIDE
    return ahead, behind


PLANE_STEPS = (10, 5, 15, 7, 13, 6, 14, 9, 11, 2, 8, 1, 3, 4, 12)
COLUMN_STEPS = (4, 5, 2, 3, 6, 7, 1)


def greet(column, plane):
    barrier = pltpu.get_barrier_semaphore()
    dp, ep = lax.axis_index("dp"), lax.axis_index("expert")
    count = 0
    for step in column:
        pl.semaphore_signal(barrier, inc=1, device_id=(column_peer(step)[0], ep), device_id_type=MESH)
        count += 1
    for step in plane:
        pl.semaphore_signal(barrier, inc=1, device_id=(dp, plane_peer(step)[0]), device_id_type=MESH)
        count += 1
    pl.semaphore_wait(barrier, count)


def to_column(step, src, dst, send, recv):
    return pltpu.make_async_remote_copy(
        src_ref=src, dst_ref=dst, send_sem=send, recv_sem=recv,
        device_id=(column_peer(step)[0], lax.axis_index("expert")), device_id_type=MESH,
    )


def to_plane(step, src, dst, send, recv):
    return pltpu.make_async_remote_copy(
        src_ref=src, dst_ref=dst, send_sem=send, recv_sem=recv,
        device_id=(lax.axis_index("dp"), plane_peer(step)[0]), device_id_type=MESH,
    )


def gather_kernel(tok, grd, meta, tok_all, grd_all, meta_all, send, recv, fsend, frecv, local):
    me = lax.axis_index("dp")
    greet((2, 4, 6, 1), ())
    pairs = ((meta, meta_all), (tok, tok_all), (grd, grd_all))
    copies = []
    for i, (src, dst) in enumerate(pairs):
        for n, step in enumerate((4, 2, 6, 1)):
            copy = to_column(step, src, dst.at[me], send.at[i, n], recv.at[i, n])
            copy.start()
            copies.append(copy)
    locals_ = []
    for i, (src, dst) in enumerate(pairs):
        copy = pltpu.make_async_copy(src, dst.at[me], local.at[i])
        copy.start()
        locals_.append(copy)
    forwards = []
    for i, (src, dst) in enumerate(pairs):
        for n, step in ((1, 2), (2, 6), (0, 4)):
            behind = column_peer(step)[1]
            copies[4 * i + n].wait_recv()
            copy = to_column(1, dst.at[behind], dst.at[behind], fsend.at[i, n], frecv.at[i, n])
            copy.start()
            forwards.append(copy)
    for i in range(3):
        copies[4 * i + 3].wait_recv()
    for copy in copies:
        copy.wait_send()
    for copy in forwards:
        copy.wait()
    for copy in locals_:
        copy.wait()


def gather_column(tok, grd, meta):
    return pl.pallas_call(
        gather_kernel,
        out_shape=[
            jax.ShapeDtypeStruct((DP,) + tok.shape, tok.dtype),
            jax.ShapeDtypeStruct((DP,) + grd.shape, grd.dtype),
            jax.ShapeDtypeStruct((DP,) + meta.shape, meta.dtype),
        ],
        in_specs=[ANY] * 3,
        out_specs=[ANY] * 3,
        scratch_shapes=[
            pltpu.SemaphoreType.DMA((3, 4)),
            pltpu.SemaphoreType.DMA((3, 4)),
            pltpu.SemaphoreType.DMA((3, 3)),
            pltpu.SemaphoreType.DMA((3, 3)),
            pltpu.SemaphoreType.DMA((3,)),
        ],
        compiler_params=pltpu.CompilerParams(collective_id=0, has_side_effects=True),
        name="gather_column",
    )(tok, grd, meta)


def exchange_kernel(a, b, p, q, r, a_out, b_out, p_out, q_out, r_out,
                    psend, precv, csend, crecv, local):
    dp, ep = lax.axis_index("dp"), lax.axis_index("expert")
    greet(COLUMN_STEPS, PLANE_STEPS)
    copies = []
    for n, step in enumerate(COLUMN_STEPS):
        target = column_peer(step)[0]
        for i, (src, dst) in enumerate(((p, p_out), (q, q_out), (r, r_out))):
            copies.append(to_column(step, src.at[target], dst.at[dp], csend.at[i, n], crecv.at[i, n]))
    for i, (src, dst) in enumerate(((a, a_out), (b, b_out))):
        for n, step in enumerate(PLANE_STEPS):
            target = plane_peer(step)[0]
            copies.append(to_plane(step, src.at[:, target], dst.at[ep], psend.at[i, n], precv.at[i, n]))
    for i, (src, dst) in enumerate(((p, p_out), (q, q_out), (r, r_out))):
        copies.append(pltpu.make_async_copy(src.at[dp], dst.at[dp], local.at[i]))
    for i, (src, dst) in enumerate(((a, a_out), (b, b_out))):
        copies.append(pltpu.make_async_copy(src.at[:, ep], dst.at[ep], local.at[3 + i]))
    for copy in copies:
        copy.start()
    for copy in copies:
        copy.wait()


def exchange(a, b, p, q, r):
    width = a.shape[-1]
    dma = pltpu.SemaphoreType.DMA
    return pl.pallas_call(
        exchange_kernel,
        out_shape=[jax.ShapeDtypeStruct((EP, DP, CAP, width), BF16)] * 2
        + [jax.ShapeDtypeStruct(p.shape, BF16)] * 3,
        in_specs=[ANY] * 5,
        out_specs=[ANY] * 5,
        scratch_shapes=[dma((2, EP - 1)), dma((2, EP - 1)), dma((3, DP - 1)), dma((3, DP - 1)), dma((5,))],
        compiler_params=pltpu.CompilerParams(collective_id=1, has_side_effects=True),
        name="exchange",
    )(a, b, p, q, r)


def scatter_kernel(a, b, a_out, b_out, own, other, summed, xsend, xrecv, zsend, zrecv, local):
    me = lax.axis_index("dp")
    z, core = me // 2, me % 2
    greet((2, 4, 6, 1), ())
    pairs = ((a, a_out), (b, b_out))
    first, kept = [], []
    for i, (src, _) in enumerate(pairs):
        copy = to_column(1, src.at[:, 1 - core], other.at[i], xsend.at[i], xrecv.at[i])
        copy.start()
        first.append(copy)
        copy = pltpu.make_async_copy(src.at[:, core], own.at[i], local.at[i])
        copy.start()
        kept.append(copy)
    last = []
    for i, (_, dst) in enumerate(pairs):
        first[i].wait_recv()
        kept[i].wait()
        for part in range(SIDE):
            summed[i, part] = (own[i, part].astype(F32) + other[i, part].astype(F32)).astype(BF16)
        for n, step in enumerate((4, 2, 6)):
            copy = to_column(step, summed.at[i, (z + step // 2) % SIDE], dst.at[n], zsend.at[i, n], zrecv.at[i, n])
            copy.start()
            last.append(copy)
        copy = pltpu.make_async_copy(summed.at[i, z], dst.at[3], local.at[2 + i])
        copy.start()
        last.append(copy)
    for copy in last:
        copy.wait()
    for copy in first:
        copy.wait_send()


def scatter_column(a, b):
    _, tok, width = a.shape
    a, b = (v.reshape(SIDE, 2, tok, width) for v in (a, b))
    return pl.pallas_call(
        scatter_kernel,
        out_shape=[jax.ShapeDtypeStruct((SIDE, tok, width), BF16)] * 2,
        in_specs=[ANY] * 2,
        out_specs=[ANY] * 2,
        scratch_shapes=[pltpu.VMEM((2, SIDE, tok, width), BF16)] * 3
        + [
            pltpu.SemaphoreType.DMA((2,)),
            pltpu.SemaphoreType.DMA((2,)),
            pltpu.SemaphoreType.DMA((2, 3)),
            pltpu.SemaphoreType.DMA((2, 3)),
            pltpu.SemaphoreType.DMA((4,)),
        ],
        compiler_params=pltpu.CompilerParams(
            collective_id=3, has_side_effects=True, vmem_limit_bytes=40 * 2**20
        ),
        name="scatter_column",
    )(a, b)


NT = (((1,), (1,)), ((), ()))
TN = (((0,), (0,)), ((), ()))


def dot(a, b, dims=(((1,), (0,)), ((), ()))):
    return lax.dot_general(a, b, dims, preferred_element_type=F32)


ORDER_Y = sum((step // SIDE) << (2 * n) for n, step in enumerate(PLANE_STEPS))
ORDER_X = sum((step % SIDE) << (2 * n) for n, step in enumerate(PLANE_STEPS))
ORDER_COLUMN = sum(step << (3 * n) for n, step in enumerate(COLUMN_STEPS))
GROUP = 2
ROWS = DP * CAP
SLAB = 256


def ordered_plane(n):
    me = lax.axis_index("expert")
    y, x = me // SIDE, me % SIDE
    dy, dx = (ORDER_Y >> (2 * n)) & 3, (ORDER_X >> (2 * n)) & 3
    ahead = ((y + dy) % SIDE) * SIDE + (x + dx) % SIDE
    behind = ((y + SIDE - dy) % SIDE) * SIDE + (x + SIDE - dx) % SIDE
    return ahead, behind


def ordered_column(n):
    me = lax.axis_index("dp")
    z, core = me // 2, me % 2
    step = (ORDER_COLUMN >> (3 * n)) & 7
    dz, other = step // 2, (core + step % 2) % 2
    return ((z + dz) % SIDE) * 2 + other, ((z + SIDE - dz) % SIDE) * 2 + other


def expert_kernel(
    x, u, wg, wu, wd, out_back, rg_back, dg, du, dd,
    wgv, wuv, wdv, hid, gg, ug, rows_in, slabs, out_v, rg_v,
    psend, precv, csend, crecv, wload, rload, sload,
):
    dp, ep = lax.axis_index("dp"), lax.axis_index("expert")
    weights = [
        pltpu.make_async_copy(src, dst, wload.at[i])
        for i, (src, dst) in enumerate(((wg, wgv), (wu, wuv), (wd, wdv)))
    ]

    def row_loads(n, slot):
        loads = []
        for part in range(GROUP):
            source = ordered_plane(n * GROUP + part)[0]
            for i, src in enumerate((x, u)):
                loads.append(pltpu.make_async_copy(
                    src.at[pl.ds(pl.multiple_of(source * ROWS, ROWS), ROWS)],
                    rows_in.at[i, slot, pl.ds(part * ROWS, ROWS)],
                    rload.at[i, slot, part],
                ))
        return loads

    def slab_loads(n, slot):
        column = pl.multiple_of(ordered_column(n)[0] * SLAB, SLAB)
        return [
            pltpu.make_async_copy(src.at[:, pl.ds(column, SLAB)], slabs.at[i, slot], sload.at[i, slot])
            for i, src in enumerate((x, u))
        ]

    def returns(n):
        target = ordered_plane(n)[0]
        return [
            pltpu.make_async_remote_copy(
                src_ref=src.at[target], dst_ref=dst.at[:, ep],
                send_sem=psend.at[i, n], recv_sem=precv.at[i, n],
                device_id=(dp, target), device_id_type=MESH,
            )
            for i, (src, dst) in enumerate(((out_v, out_back), (rg_v, rg_back)))
        ]

    def own_returns():
        return [
            pltpu.make_async_copy(src.at[ep], dst.at[:, ep], psend.at[i, EP - 1])
            for i, (src, dst) in enumerate(((out_v, out_back), (rg_v, rg_back)))
        ]

    def slices():
        return ((wgv, dg), (wuv, du), (wdv, dd))

    def grads(n):
        target = ordered_column(n)[0]
        part = pl.ds(pl.multiple_of(target * SLAB, SLAB), SLAB)
        return [
            pltpu.make_async_remote_copy(
                src_ref=src.at[part], dst_ref=dst.at[dp],
                send_sem=csend.at[i, n], recv_sem=crecv.at[i, n],
                device_id=(target, ep), device_id_type=MESH,
            )
            for i, (src, dst) in enumerate(slices())
        ]

    def own_grads():
        part = pl.ds(pl.multiple_of(dp * SLAB, SLAB), SLAB)
        return [
            pltpu.make_async_copy(src.at[part], dst.at[dp], csend.at[i, DP - 1])
            for i, (src, dst) in enumerate(slices())
        ]

    for copy in weights + row_loads(0, 0):
        copy.start()
    greet(COLUMN_STEPS, PLANE_STEPS)
    for copy in weights:
        copy.wait()

    groups = EP // GROUP

    @pl.loop(0, groups)
    def _(n):
        slot = n % 2
        for copy in row_loads(n, slot):
            copy.wait()

        @pl.when(n + 1 < groups)
        def _():
            for copy in row_loads(n + 1, 1 - slot):
                copy.start()

        xb, ub = rows_in[0, slot], rows_in[1, slot]
        gate, up = dot(xb, wgv[...]), dot(xb, wuv[...])
        s = jax.nn.sigmoid(gate)
        hidden = (gate * s * up).astype(BF16)
        out = dot(hidden, wdv[...], NT).astype(BF16)
        hg = dot(ub, wdv[...])
        gate_grad = (hg * up * s * (1.0 + gate * (1.0 - s))).astype(BF16)
        up_grad = (hg * gate * s).astype(BF16)
        rg = (dot(gate_grad, wgv[...], NT) + dot(up_grad, wuv[...], NT)).astype(BF16)
        for part in range(GROUP):
            source = ordered_plane(n * GROUP + part)[0]
            these = slice(part * ROWS, (part + 1) * ROWS)
            out_v[source] = out[these].reshape(DP, CAP, -1)
            rg_v[source] = rg[these].reshape(DP, CAP, -1)
            held = pl.ds(pl.multiple_of(source * ROWS, ROWS), ROWS)
            hid[held], gg[held], ug[held] = hidden[these], gate_grad[these], up_grad[these]
        for part in range(GROUP - 1):
            for copy in returns(n * GROUP + part):
                copy.start()

        @pl.when(n + 1 < groups)
        def _():
            for copy in returns(n * GROUP + GROUP - 1):
                copy.start()

        @pl.when(n + 1 == groups)
        def _():
            for copy in own_returns() + slab_loads(0, 0):
                copy.start()

    @pl.loop(0, DP)
    def _(n):
        slot = n % 2
        for copy in slab_loads(n, slot):
            copy.wait()

        @pl.when(n + 1 < DP)
        def _():
            for copy in slab_loads(n + 1, 1 - slot):
                copy.start()

        part = pl.ds(pl.multiple_of(ordered_column(n)[0] * SLAB, SLAB), SLAB)
        wgv[part] = dot(slabs[0, slot], gg[...], TN).astype(BF16)
        wuv[part] = dot(slabs[0, slot], ug[...], TN).astype(BF16)
        wdv[part] = dot(slabs[1, slot], hid[...], TN).astype(BF16)

        @pl.when(n + 1 < DP)
        def _():
            for copy in grads(n):
                copy.start()

        @pl.when(n + 1 == DP)
        def _():
            for copy in own_grads():
                copy.start()

    for copy in own_returns() + own_grads():
        copy.wait()

    @pl.loop(0, DP - 1)
    def _(n):
        for copy in grads(n):
            copy.wait()

    @pl.loop(0, EP - 1)
    def _(n):
        for copy in returns(n):
            copy.wait()


def expert(x, u, wg, wu, wd):
    rows, width = x.shape
    ff = wg.shape[1]
    dma = pltpu.SemaphoreType.DMA
    return pl.pallas_call(
        expert_kernel,
        out_shape=[jax.ShapeDtypeStruct((DP, EP, CAP, width), BF16)] * 2
        + [jax.ShapeDtypeStruct((DP, width // DP, ff), BF16)] * 3,
        in_specs=[ANY] * 5,
        out_specs=[ANY] * 5,
        scratch_shapes=[pltpu.VMEM((width, ff), BF16)] * 3
        + [pltpu.VMEM((rows, ff), BF16)] * 3
        + [
            pltpu.VMEM((2, 2, GROUP * ROWS, width), BF16),
            pltpu.VMEM((2, 2, rows, SLAB), BF16),
            pltpu.VMEM((EP, DP, CAP, width), BF16),
            pltpu.VMEM((EP, DP, CAP, width), BF16),
            dma((2, EP)), dma((2, EP)), dma((3, DP)), dma((3, DP)),
            dma((3,)), dma((2, 2, GROUP)), dma((2, 2)),
        ],
        compiler_params=pltpu.CompilerParams(
            collective_id=2, has_side_effects=True, vmem_limit_bytes=62 * 2**20
        ),
        name="expert",
    )(x, u, wg, wu, wd)


def local(tokens, expert_ids, gate_codes, grad_out, w_gate, w_up, w_down):
    dp = lax.axis_index("dp")
    tok, width = tokens.shape
    ff = w_gate.shape[-1]
    meta = (expert_ids * 256 + gate_codes).T
    tok_all, grd_all, meta_all = gather_column(tokens, grad_out, meta)
    ids, codes = meta_all // 256, meta_all % 256
    mine = jnp.arange(EP, dtype=jnp.int32) * DP + dp
    named = ids[:, None] == mine[None, :, None, None]
    has = jnp.any(named, axis=2)
    gate = jnp.sum(jnp.where(named, codes[:, None], 0), axis=2).astype(F32) / 256.0
    earlier = jnp.triu(jnp.ones((tok, tok), BF16), 1)
    rank = jnp.dot(has.astype(BF16), earlier, preferred_element_type=F32).astype(jnp.int32)
    slot = jnp.where(has, rank, -1)[:, :, None, :]
    pick = slot == jnp.arange(CAP, dtype=jnp.int32)[None, None, :, None]
    weight = jnp.where(pick, gate[:, :, None, :], 0.0).astype(BF16).reshape(DP, EP * CAP, tok)
    pick = pick.astype(BF16).reshape(DP, EP * CAP, tok)
    gathers = (((2,), (1,)), ((0,), (0,)))
    sends = (((1,), (1,)), ((0,), (0,)))

    def spread(matrix, rows):
        picked = lax.dot_general(matrix, rows, gathers, preferred_element_type=F32)
        return picked.astype(BF16).reshape(DP, EP, CAP, width)

    def collect(matrix, rows):
        summed = lax.dot_general(
            matrix, rows.reshape(DP, EP * CAP, width), sends, preferred_element_type=F32
        )
        return summed.astype(BF16)

    x, u, wg, wu, wd = exchange(
        spread(pick, tok_all), spread(weight, grd_all), w_gate, w_up, w_down
    )
    x, u = x.reshape(-1, width), u.reshape(-1, width)
    wg, wu, wd = (w.reshape(width, ff) for w in (wg, wu, wd))
    out, rg, dg, du, dd = expert(x, u, wg, wu, wd)
    mixed, tokens_grad = scatter_column(collect(weight, out), collect(pick, rg))
    mixed, tokens_grad = (
        jnp.sum(v.astype(F32), axis=0).astype(BF16) for v in (mixed, tokens_grad)
    )
    return mixed, tokens_grad, dg, du, dd


def solution(mesh):
    rows, weights = P(("dp", "expert"), None), P("expert", "dp", None)
    return jax.shard_map(
        local,
        mesh=mesh,
        in_specs=(rows,) * 4 + (weights,) * 3,
        out_specs=(rows,) * 2 + (weights,) * 3,
        check_vma=False,
    )
```

```python
import jax
import jax.numpy as jnp
from jax import lax
from jax.experimental import pallas as pl
from jax.experimental.pallas import tpu as pltpu
from jax.sharding import PartitionSpec as P

BF16 = jnp.bfloat16
F32 = jnp.float32
MESH = pl.DeviceIdType.MESH
ANY = pl.BlockSpec(memory_space=pl.ANY)
VMEM = pl.BlockSpec(memory_space=pltpu.VMEM)
DP = 8
EP = 16
SIDE = 4
CAP = 16
TOK = 128


def column_peer(step):
    me = lax.axis_index("dp")
    z, core = me // 2, me % 2
    dz, other = step // 2, (core + step % 2) % 2
    return ((z + dz) % SIDE) * 2 + other, ((z + SIDE - dz) % SIDE) * 2 + other


def plane_peer(step):
    me = lax.axis_index("expert")
    y, x = me // SIDE, me % SIDE
    dy, dx = step // SIDE, step % SIDE
    ahead = ((y + dy) % SIDE) * SIDE + (x + dx) % SIDE
    behind = ((y + SIDE - dy) % SIDE) * SIDE + (x + SIDE - dx) % SIDE
    return ahead, behind


PLANE_STEPS = (1, 3, 4, 12, 5, 15, 7, 13, 10, 2, 8, 6, 14, 9, 11)
COLUMN_STEPS = (4, 5, 2, 3, 6, 7, 1)


def greet(column, plane):
    barrier = pltpu.get_barrier_semaphore()
    dp, ep = lax.axis_index("dp"), lax.axis_index("expert")
    count = 0
    for step in column:
        pl.semaphore_signal(barrier, inc=1, device_id=(column_peer(step)[0], ep), device_id_type=MESH)
        count += 1
    for step in plane:
        pl.semaphore_signal(barrier, inc=1, device_id=(dp, plane_peer(step)[0]), device_id_type=MESH)
        count += 1
    pl.semaphore_wait(barrier, count)


def to_column(step, src, dst, send, recv):
    return pltpu.make_async_remote_copy(
        src_ref=src, dst_ref=dst, send_sem=send, recv_sem=recv,
        device_id=(column_peer(step)[0], lax.axis_index("expert")), device_id_type=MESH,
    )


def to_plane(step, src, dst, send, recv):
    return pltpu.make_async_remote_copy(
        src_ref=src, dst_ref=dst, send_sem=send, recv_sem=recv,
        device_id=(lax.axis_index("dp"), plane_peer(step)[0]), device_id_type=MESH,
    )


def gather_kernel(tok, meta, tok_all, meta_all, send, recv, fsend, frecv, local):
    me = lax.axis_index("dp")
    greet((2, 4, 6, 1), ())
    pairs = ((meta, meta_all), (tok, tok_all))
    copies = []
    for i, (src, dst) in enumerate(pairs):
        for n, step in enumerate((4, 2, 6, 1)):
            copy = to_column(step, src, dst.at[me], send.at[i, n], recv.at[i, n])
            copy.start()
            copies.append(copy)
    locals_ = []
    for i, (src, dst) in enumerate(pairs):
        copy = pltpu.make_async_copy(src, dst.at[me], local.at[i])
        copy.start()
        locals_.append(copy)
    forwards = []
    for i, (src, dst) in enumerate(pairs):
        for n, step in ((1, 2), (2, 6), (0, 4)):
            behind = column_peer(step)[1]
            copies[4 * i + n].wait_recv()
            copy = to_column(1, dst.at[behind], dst.at[behind], fsend.at[i, n], frecv.at[i, n])
            copy.start()
            forwards.append(copy)
    for i in range(2):
        copies[4 * i + 3].wait_recv()
    for copy in copies:
        copy.wait_send()
    for copy in forwards:
        copy.wait()
    for copy in locals_:
        copy.wait()


def gather_column(tok, meta):
    dma = pltpu.SemaphoreType.DMA
    return pl.pallas_call(
        gather_kernel,
        out_shape=[
            jax.ShapeDtypeStruct((DP,) + tok.shape, tok.dtype),
            jax.ShapeDtypeStruct((DP,) + meta.shape, meta.dtype),
        ],
        in_specs=[ANY] * 2,
        out_specs=[ANY] * 2,
        scratch_shapes=[dma((2, 4)), dma((2, 4)), dma((2, 3)), dma((2, 3)), dma((2,))],
        compiler_params=pltpu.CompilerParams(collective_id=0, has_side_effects=True),
        name="gather_column",
    )(tok, meta)


PEERS = EP - 1
SENDS = DP * PEERS
WINDOW = 24
HALF = DP // 2


def exchange_kernel(tok_all, grd, pick, weight, p, q, r, a_out, b_out, p_out, q_out, r_out,
                    grd_all, tok_rows, grd_rows,
                    psend, precv, csend, crecv, gsend, grecv, fsend, frecv, local):
    dp, ep = lax.axis_index("dp"), lax.axis_index("expert")
    greet(COLUMN_STEPS, PLANE_STEPS)
    gathers = [
        to_column(step, grd, grd_all.at[dp], gsend.at[n], grecv.at[n]) for n, step in enumerate((4, 2, 6, 1))
    ]
    own = pltpu.make_async_copy(grd, grd_all.at[dp], local.at[5])
    columns = []
    for n, step in enumerate(COLUMN_STEPS):
        target = column_peer(step)[0]
        for i, (src, dst) in enumerate(((p, p_out), (q, q_out), (r, r_out))):
            columns.append(to_column(step, src.at[target], dst.at[dp], csend.at[i, n], crecv.at[i, n]))
    for i, (src, dst) in enumerate(((p, p_out), (q, q_out), (r, r_out))):
        columns.append(pltpu.make_async_copy(src.at[dp], dst.at[dp], local.at[i]))
    own_rows = [
        pltpu.make_async_copy(src.at[ep], dst.at[ep], local.at[3 + i])
        for i, (src, dst) in enumerate(((tok_rows, a_out), (grd_rows, b_out)))
    ]
    ends = ((tok_rows, a_out), (grd_rows, b_out))

    def plane(i, k):
        src, dst = ends[i]
        target, part = ordered_plane(k % PEERS)[0], k // PEERS
        return pltpu.make_async_remote_copy(
            src_ref=src.at[target, part], dst_ref=dst.at[ep, part],
            send_sem=psend.at[i, k], recv_sem=precv.at[i, k],
            device_id=(dp, target), device_id_type=MESH,
        )

    def go_on(i, start, stop):
        @pl.loop(start, stop)
        def _(k):
            plane(i, k - WINDOW).wait_send()
            plane(i, k).start()

    def spread(matrix, rows, result, start, stop):
        @pl.loop(start, stop)
        def _(source):
            picked = dot(matrix[source], rows[source]).astype(BF16)
            result[:, source] = picked.reshape(EP, CAP, picked.shape[-1])

    for copy in gathers + [own]:
        copy.start()
    spread(pick, tok_all, tok_rows, 0, HALF)

    @pl.loop(0, WINDOW)
    def _(k):
        plane(0, k).start()

    spread(pick, tok_all, tok_rows, HALF, DP)
    own_rows[0].start()
    go_on(0, WINDOW, 56)
    forwards = []
    for n, step in ((1, 2), (2, 6), (0, 4)):
        behind = column_peer(step)[1]
        gathers[n].wait_recv()
        copy = to_column(1, grd_all.at[behind], grd_all.at[behind], fsend.at[n], frecv.at[n])
        copy.start()
        forwards.append(copy)
    for copy in columns:
        copy.start()
    go_on(0, 56, 100)
    gathers[3].wait_recv()
    for copy in forwards:
        copy.wait_recv()
    own.wait()
    spread(weight, grd_all, grd_rows, 0, DP)
    own_rows[1].start()
    go_on(0, 100, SENDS)

    @pl.loop(0, WINDOW)
    def _(k):
        plane(0, SENDS - WINDOW + k).wait_send()
        plane(1, k).start()

    go_on(1, WINDOW, SENDS)

    @pl.loop(SENDS - WINDOW, SENDS)
    def _(k):
        plane(1, k).wait_send()

    for i in range(2):

        @pl.loop(0, SENDS)
        def _(k):
            plane(i, k).wait_recv()

    for copy in gathers + forwards:
        copy.wait_send()
    for copy in columns + own_rows:
        copy.wait()


def exchange(tok_all, grd, pick, weight, p, q, r):
    tok, width = grd.shape
    dma = pltpu.SemaphoreType.DMA
    rows = (EP, DP, CAP, width)
    return pl.pallas_call(
        exchange_kernel,
        out_shape=[jax.ShapeDtypeStruct(rows, BF16)] * 2 + [jax.ShapeDtypeStruct(p.shape, BF16)] * 3,
        in_specs=[VMEM, ANY, VMEM, VMEM, ANY, ANY, ANY],
        out_specs=[ANY] * 5,
        scratch_shapes=[
            pltpu.VMEM((DP, tok, width), BF16),
            pltpu.VMEM(rows, BF16),
            pltpu.VMEM(rows, BF16),
            dma((2, SENDS)), dma((2, SENDS)), dma((3, DP - 1)), dma((3, DP - 1)),
            dma((4,)), dma((4,)), dma((3,)), dma((3,)), dma((6,)),
        ],
        compiler_params=pltpu.CompilerParams(
            collective_id=1, has_side_effects=True, vmem_limit_bytes=63 * 2**20
        ),
        name="exchange",
    )(tok_all, grd, pick, weight, p, q, r)


NT = (((1,), (1,)), ((), ()))
TN = (((0,), (0,)), ((), ()))


def dot(a, b, dims=(((1,), (0,)), ((), ()))):
    return lax.dot_general(a, b, dims, preferred_element_type=F32)


ORDER_Y = sum((step // SIDE) << (2 * n) for n, step in enumerate(PLANE_STEPS))
ORDER_X = sum((step % SIDE) << (2 * n) for n, step in enumerate(PLANE_STEPS))
ORDER_COLUMN = sum(step << (3 * n) for n, step in enumerate(COLUMN_STEPS))
GROUP = 2
ROWS = DP * CAP
SLAB = 256


def ordered_plane(n):
    me = lax.axis_index("expert")
    y, x = me // SIDE, me % SIDE
    dy, dx = (ORDER_Y >> (2 * n)) & 3, (ORDER_X >> (2 * n)) & 3
    ahead = ((y + dy) % SIDE) * SIDE + (x + dx) % SIDE
    behind = ((y + SIDE - dy) % SIDE) * SIDE + (x + SIDE - dx) % SIDE
    return ahead, behind


def ordered_column(n):
    me = lax.axis_index("dp")
    z, core = me // 2, me % 2
    step = (ORDER_COLUMN >> (3 * n)) & 7
    dz, other = step // 2, (core + step % 2) % 2
    return ((z + dz) % SIDE) * 2 + other, ((z + SIDE - dz) % SIDE) * 2 + other


def expert_kernel(
    x, u, wg, wu, wd, weight, pick, mixed, tokens_grad, out_back, rg_back, dg, du, dd,
    wgv, wuv, wdv, hid, gg, ug, rows_in, slabs, out_v, rg_v, paired, arrived,
    psend, precv, csend, crecv, wload, rload, sload, own, bload, xsend, xrecv, zsend, zrecv,
):
    dp, ep = lax.axis_index("dp"), lax.axis_index("expert")
    z, core = dp // 2, dp % 2
    weights = [
        pltpu.make_async_copy(src, dst, wload.at[i])
        for i, (src, dst) in enumerate(((wg, wgv), (wu, wuv), (wd, wdv)))
    ]
    backs = ((out_v, out_back), (rg_v, rg_back))

    def ahead(n):
        return (0b00110110 >> (2 * n)) & 3

    def row_loads(n, slot):
        loads = []
        for part in range(GROUP):
            source = ordered_plane(n * GROUP + part)[0]
            for i, src in enumerate((x, u)):
                loads.append(pltpu.make_async_copy(
                    src.at[source], rows_in.at[i, slot, pl.ds(part * DP, DP)], rload.at[i, slot, part]
                ))
        return loads

    def slab_loads(n, slot):
        column = pl.multiple_of(ordered_column(n)[0] * SLAB, SLAB)
        return [
            pltpu.make_async_copy(src.at[:, :, :, pl.ds(column, SLAB)], slabs.at[i, slot], sload.at[i, slot])
            for i, src in enumerate((x, u))
        ]

    def back(i, k):
        src, dst = backs[i]
        n, part = (k // DP, k % DP) if i == 0 else (k % PEERS, k // PEERS)
        target = ordered_plane(n)[0]
        part = (z + ahead(part // 2)) % SIDE * 2 + part % 2
        return pltpu.make_async_remote_copy(
            src_ref=src.at[target, part], dst_ref=dst.at[ep, part],
            send_sem=psend.at[i, k], recv_sem=precv.at[i, k],
            device_id=(dp, target), device_id_type=MESH,
        )

    def own_back(i):
        return pltpu.make_async_copy(backs[i][0].at[ep], backs[i][1].at[ep], own.at[i])

    slices = ((wgv, dg), (wuv, du), (wdv, dd))

    def grads(n):
        target = ordered_column(n)[0]
        part = pl.ds(pl.multiple_of(target * SLAB, SLAB), SLAB)
        return [
            pltpu.make_async_remote_copy(
                src_ref=src.at[part], dst_ref=dst.at[dp],
                send_sem=csend.at[i, n], recv_sem=crecv.at[i, n],
                device_id=(target, ep), device_id_type=MESH,
            )
            for i, (src, dst) in enumerate(slices)
        ]

    def own_grads():
        part = pl.ds(pl.multiple_of(dp * SLAB, SLAB), SLAB)
        return [
            pltpu.make_async_copy(src.at[part], dst.at[dp], own.at[2 + i])
            for i, (src, dst) in enumerate(slices)
        ]

    def back_load(i, source, slot):
        return pltpu.make_async_copy(backs[i][1].at[:, source], rows_in.at[0, slot], bload.at[slot])

    def pair_copy(i, n):
        place = ((z + ahead(n)) % SIDE) * 2 + 1 - core
        return to_column(1, out_v.at[place], paired.at[i, n], xsend.at[i, n], xrecv.at[i, n])

    def z_copy(i, n):
        place = ((z + ahead(n)) % SIDE) * 2 + core
        return to_column(2 * ahead(n), out_v.at[place], arrived.at[i, n], zsend.at[i, n], zrecv.at[i, n])

    def collect(i, matrix, n):
        chip = (z + ahead(n)) % SIDE
        places = (chip * 2 + 1 - core, chip * 2 + core)
        for slot in range(2):
            back_load(i, places[slot], slot).start()
        for slot in range(2):
            back_load(i, places[slot], slot).wait()
            held = rows_in[0, slot]
            summed = dot(matrix[places[slot]], held.reshape(EP * CAP, held.shape[-1]), TN).astype(BF16)
            out_v[places[slot]] = summed.reshape(out_v.shape[1:])
            if slot == 0:
                pair_copy(i, n).start()

    def add_pair(i, n):
        place = ((z + ahead(n)) % SIDE) * 2 + core
        pair_copy(i, n).wait_recv()
        out_v[place] = (out_v[place].astype(F32) + paired[i, n].astype(F32)).astype(BF16)
        if n < SIDE - 1:
            z_copy(i, n).start()

    def finish(i, result):
        total = out_v[dp].astype(F32)
        for n in range(SIDE - 1):
            z_copy(i, n).wait_recv()
            total += arrived[i, n].astype(F32)
        result[...] = total.astype(BF16).reshape(result.shape)
        for n in range(SIDE):
            pair_copy(i, n).wait_send()
        for n in range(SIDE - 1):
            z_copy(i, n).wait_send()

    for copy in weights + row_loads(0, 0):
        copy.start()
    greet(COLUMN_STEPS, PLANE_STEPS)
    for copy in weights:
        copy.wait()

    groups = EP // GROUP

    @pl.loop(0, groups)
    def _(n):
        slot = n % 2
        for copy in row_loads(n, slot):
            copy.wait()

        @pl.when(n + 1 < groups)
        def _():
            for copy in row_loads(n + 1, 1 - slot):
                copy.start()

        shape = (GROUP * ROWS, rows_in.shape[-1])
        xb, ub = rows_in[0, slot].reshape(shape), rows_in[1, slot].reshape(shape)
        gate, up = dot(xb, wgv[...]), dot(xb, wuv[...])
        s = jax.nn.sigmoid(gate)
        hidden = (gate * s * up).astype(BF16)
        out = dot(hidden, wdv[...], NT).astype(BF16)
        hg = dot(ub, wdv[...])
        gate_grad = (hg * up * s * (1.0 + gate * (1.0 - s))).astype(BF16)
        up_grad = (hg * gate * s).astype(BF16)
        rg = (dot(gate_grad, wgv[...], NT) + dot(up_grad, wuv[...], NT)).astype(BF16)
        for part in range(GROUP):
            source = ordered_plane(n * GROUP + part)[0]
            these = slice(part * ROWS, (part + 1) * ROWS)
            out_v[source] = out[these].reshape(DP, CAP, -1)
            rg_v[source] = rg[these].reshape(DP, CAP, -1)
            held = pl.ds(pl.multiple_of(source * ROWS, ROWS), ROWS)
            hid[held], gg[held], ug[held] = hidden[these], gate_grad[these], up_grad[these]
        @pl.loop(0, 12)
        def _(j):
            back(0, n * 12 + j).start()

    first = 12 * groups

    for i in range(2):
        own_back(i).start()
    for copy in slab_loads(0, 0):
        copy.start()

    @pl.loop(0, DP)
    def _(n):
        slot = n % 2
        for copy in slab_loads(n, slot):
            copy.wait()

        @pl.when(n + 1 < DP)
        def _():
            for copy in slab_loads(n + 1, 1 - slot):
                copy.start()

        part = pl.ds(pl.multiple_of(ordered_column(n)[0] * SLAB, SLAB), SLAB)
        shape = (EP * ROWS, SLAB)
        wgv[part] = dot(slabs[0, slot].reshape(shape), gg[...], TN).astype(BF16)
        wuv[part] = dot(slabs[0, slot].reshape(shape), ug[...], TN).astype(BF16)
        wdv[part] = dot(slabs[1, slot].reshape(shape), hid[...], TN).astype(BF16)

        @pl.when(n + 1 < DP)
        def _():
            for copy in grads(n):
                copy.start()

        @pl.when(n + 1 == DP)
        def _():
            for copy in own_grads():
                copy.start()

        @pl.when(n < (SENDS - first) // 4)
        def _():
            for j in range(4):
                back(0, first - WINDOW + 4 * n + j).wait_send()
                back(0, first + 4 * n + j).start()

    @pl.loop(0, WINDOW)
    def _(k):
        back(0, SENDS - WINDOW + k).wait_send()
        back(1, k).start()

    def go_on(start, stop):
        @pl.loop(start, stop)
        def _(k):
            back(1, k - WINDOW).wait_send()
            back(1, k).start()

    go_on(WINDOW, 56)

    @pl.loop(0, first - WINDOW)
    def _(k):
        back(0, k).wait_send()

    @pl.loop(0, SENDS)
    def _(k):
        back(0, k).wait_recv()

    own_back(0).wait()
    for n in range(SIDE):
        collect(0, weight, n)
    go_on(56, 80)
    for n in range(SIDE):
        add_pair(0, n)
    go_on(80, 104)
    finish(0, mixed)
    go_on(104, SENDS)
    own_back(1).wait()
    for n in range(SIDE):

        @pl.loop(n * 2 * PEERS, (n + 1) * 2 * PEERS)
        def _(k):
            back(1, k).wait_recv()

        collect(1, pick, n)
        if n > 0:
            add_pair(1, n - 1)
    add_pair(1, SIDE - 1)
    finish(1, tokens_grad)

    @pl.loop(SENDS - WINDOW, SENDS)
    def _(k):
        back(1, k).wait_send()

    for copy in own_grads():
        copy.wait()

    @pl.loop(0, DP - 1)
    def _(n):
        for copy in grads(n):
            copy.wait()


def expert(x, u, wg, wu, wd, weight, pick):
    width = x.shape[-1]
    ff = wg.shape[1]
    tok = weight.shape[-1]
    dma = pltpu.SemaphoreType.DMA
    block = (DP, CAP, width)
    results = pl.pallas_call(
        expert_kernel,
        out_shape=[jax.ShapeDtypeStruct((tok, width), BF16)] * 2
        + [jax.ShapeDtypeStruct((EP, DP, CAP, width), BF16)] * 2
        + [jax.ShapeDtypeStruct((DP, width // DP, ff), BF16)] * 3,
        in_specs=[ANY] * 5 + [VMEM] * 2,
        out_specs=[VMEM] * 2 + [ANY] * 5,
        scratch_shapes=[pltpu.VMEM((width, ff), BF16)] * 3
        + [pltpu.VMEM((EP * ROWS, ff), BF16)] * 3
        + [
            pltpu.VMEM((2, 2, GROUP * DP, CAP, width), BF16),
            pltpu.VMEM((2, 2, EP, DP, CAP, SLAB), BF16),
            pltpu.VMEM((EP,) + block, BF16),
            pltpu.VMEM((EP,) + block, BF16),
            pltpu.VMEM((2, SIDE) + block, BF16),
            pltpu.VMEM((2, SIDE - 1) + block, BF16),
            dma((2, SENDS)), dma((2, SENDS)), dma((3, DP - 1)), dma((3, DP - 1)),
            dma((3,)), dma((2, 2, GROUP)), dma((2, 2)), dma((5,)), dma((2,)),
            dma((2, SIDE)), dma((2, SIDE)), dma((2, SIDE - 1)), dma((2, SIDE - 1)),
        ],
        compiler_params=pltpu.CompilerParams(
            collective_id=2, has_side_effects=True, vmem_limit_bytes=63 * 2**20
        ),
        name="expert",
    )(x, u, wg, wu, wd, weight, pick)
    return results[0], results[1], *results[4:]


def local(tokens, expert_ids, gate_codes, grad_out, w_gate, w_up, w_down):
    dp = lax.axis_index("dp")
    tok, width = tokens.shape
    ff = w_gate.shape[-1]
    meta = (expert_ids * 256 + gate_codes).T
    tok_all, meta_all = gather_column(tokens, meta)
    ids, codes = meta_all // 256, meta_all % 256
    mine = jnp.arange(EP, dtype=jnp.int32) * DP + dp
    named = ids[:, None] == mine[None, :, None, None]
    has = jnp.any(named, axis=2)
    gate = jnp.sum(jnp.where(named, codes[:, None], 0), axis=2).astype(F32) / 256.0
    earlier = jnp.triu(jnp.ones((tok, tok), BF16), 1)
    rank = jnp.dot(has.astype(BF16), earlier, preferred_element_type=F32).astype(jnp.int32)
    slot = jnp.where(has, rank, -1)[:, :, None, :]
    pick = slot == jnp.arange(CAP, dtype=jnp.int32)[None, None, :, None]
    weight = jnp.where(pick, gate[:, :, None, :], 0.0).astype(BF16).reshape(DP, EP * CAP, tok)
    pick = pick.astype(BF16).reshape(DP, EP * CAP, tok)
    x, u, wg, wu, wd = exchange(tok_all, grad_out, pick, weight, w_gate, w_up, w_down)
    wg, wu, wd = (w.reshape(width, ff) for w in (wg, wu, wd))
    return expert(x, u, wg, wu, wd, weight, pick)


def solution(mesh):
    rows, weights = P(("dp", "expert"), None), P("expert", "dp", None)
    return jax.shard_map(
        local,
        mesh=mesh,
        in_specs=(rows,) * 4 + (weights,) * 3,
        out_specs=(rows,) * 2 + (weights,) * 3,
        check_vma=False,
    )
```

```python
import jax
import jax.numpy as jnp
from jax import lax
from jax.experimental import pallas as pl
from jax.experimental.pallas import tpu as pltpu
from jax.sharding import PartitionSpec as P

BF16 = jnp.bfloat16
F32 = jnp.float32
MESH = pl.DeviceIdType.MESH
ANY = pl.BlockSpec(memory_space=pl.ANY)
VMEM = pl.BlockSpec(memory_space=pltpu.VMEM)
DP = 8
EP = 16
SIDE = 4
CAP = 16
TOK = 128


def column_peer(step):
    me = lax.axis_index("dp")
    z, core = me // 2, me % 2
    dz, other = step // 2, (core + step % 2) % 2
    return ((z + dz) % SIDE) * 2 + other, ((z + SIDE - dz) % SIDE) * 2 + other


def plane_peer(step):
    me = lax.axis_index("expert")
    y, x = me // SIDE, me % SIDE
    dy, dx = step // SIDE, step % SIDE
    ahead = ((y + dy) % SIDE) * SIDE + (x + dx) % SIDE
    behind = ((y + SIDE - dy) % SIDE) * SIDE + (x + SIDE - dx) % SIDE
    return ahead, behind


PLANE_STEPS = (1, 3, 4, 12, 5, 15, 7, 13, 10, 2, 8, 6, 14, 9, 11)
COLUMN_STEPS = (4, 5, 2, 3, 6, 7, 1)


def greet(column, plane):
    barrier = pltpu.get_barrier_semaphore()
    dp, ep = lax.axis_index("dp"), lax.axis_index("expert")
    count = 0
    for step in column:
        pl.semaphore_signal(barrier, inc=1, device_id=(column_peer(step)[0], ep), device_id_type=MESH)
        count += 1
    for step in plane:
        pl.semaphore_signal(barrier, inc=1, device_id=(dp, plane_peer(step)[0]), device_id_type=MESH)
        count += 1
    pl.semaphore_wait(barrier, count)


def to_column(step, src, dst, send, recv):
    return pltpu.make_async_remote_copy(
        src_ref=src, dst_ref=dst, send_sem=send, recv_sem=recv,
        device_id=(column_peer(step)[0], lax.axis_index("expert")), device_id_type=MESH,
    )


def to_plane(step, src, dst, send, recv):
    return pltpu.make_async_remote_copy(
        src_ref=src, dst_ref=dst, send_sem=send, recv_sem=recv,
        device_id=(lax.axis_index("dp"), plane_peer(step)[0]), device_id_type=MESH,
    )


def gather_kernel(meta, meta_all, send, recv, local):
    me = lax.axis_index("dp")
    greet(COLUMN_STEPS, ())
    copies = [
        to_column(step, meta, meta_all.at[me], send.at[n], recv.at[n]) for n, step in enumerate(COLUMN_STEPS)
    ]
    copies.append(pltpu.make_async_copy(meta, meta_all.at[me], local))
    for copy in copies:
        copy.start()
    for copy in copies:
        copy.wait()


def gather_column(meta):
    dma = pltpu.SemaphoreType.DMA
    return pl.pallas_call(
        gather_kernel,
        out_shape=jax.ShapeDtypeStruct((DP,) + meta.shape, meta.dtype),
        in_specs=[ANY],
        out_specs=ANY,
        scratch_shapes=[dma((DP - 1,)), dma((DP - 1,)), dma],
        compiler_params=pltpu.CompilerParams(collective_id=0, has_side_effects=True),
        name="gather_column",
    )(meta)


PEERS = EP - 1
SENDS = DP * PEERS
WINDOW = 24


def exchange_kernel(tok, grd, pick, weight, p, q, r, a_out, b_out, p_out, q_out, r_out,
                    tok_all, grd_all, tok_rows, grd_rows,
                    psend, precv, csend, crecv, gsend, grecv, fsend, frecv, local):
    dp, ep = lax.axis_index("dp"), lax.axis_index("expert")
    z, core = dp // 2, dp % 2
    gathered = ((tok, tok_all), (grd, grd_all))

    def place(j):
        return (z + ((0b10110100 >> (j // 2 * 2)) & 3)) % SIDE * 2 + (core + j % 2) % 2

    own = [
        pltpu.make_async_copy(src, dst.at[dp], local.at[5 + i]) for i, (src, dst) in enumerate(gathered)
    ]
    own[0].start()
    greet(COLUMN_STEPS, PLANE_STEPS)
    gathers = [
        [
            to_column(step, src, dst.at[dp], gsend.at[i, n], grecv.at[i, n])
            for n, step in enumerate((1, 6, 2, 4))
        ]
        for i, (src, dst) in enumerate(gathered)
    ]

    def forward(i, m):
        block = gathered[i][1].at[place(2 * m)]
        return to_column(1, block, block, fsend.at[i, m - 1], frecv.at[i, m - 1])

    columns = []
    for n, step in enumerate(COLUMN_STEPS):
        target = column_peer(step)[0]
        for i, (src, dst) in enumerate(((p, p_out), (q, q_out), (r, r_out))):
            columns.append(to_column(step, src.at[target], dst.at[dp], csend.at[i, n], crecv.at[i, n]))
    for i, (src, dst) in enumerate(((p, p_out), (q, q_out), (r, r_out))):
        columns.append(pltpu.make_async_copy(src.at[dp], dst.at[dp], local.at[i]))
    own_rows = [
        pltpu.make_async_copy(src.at[ep], dst.at[ep], local.at[3 + i])
        for i, (src, dst) in enumerate(((tok_rows, a_out), (grd_rows, b_out)))
    ]
    ends = ((tok_rows, a_out), (grd_rows, b_out))

    def plane(i, k):
        src, dst = ends[i]
        target, part = ordered_plane(k % PEERS)[0], place(k // PEERS)
        return pltpu.make_async_remote_copy(
            src_ref=src.at[target, part], dst_ref=dst.at[ep, part],
            send_sem=psend.at[i, k], recv_sem=precv.at[i, k],
            device_id=(dp, target), device_id_type=MESH,
        )

    def go_on(i, start, stop):
        @pl.loop(start, stop)
        def _(k):
            plane(i, k - WINDOW).wait_send()
            plane(i, k).start()

    def spread(matrix, rows, result, j):
        part = place(j)
        picked = dot(matrix[part], rows[part]).astype(BF16)
        result[:, part] = picked.reshape(EP, CAP, picked.shape[-1])

    for copy in gathers[0] + gathers[1] + own[1:]:
        copy.start()
    own[0].wait()
    for m in range(SIDE):
        if m:
            gathers[0][m].wait_recv()
            forward(0, m).start()
        for j in (2 * m, 2 * m + 1):
            if j == 1:
                gathers[0][0].wait_recv()
            elif j % 2:
                forward(0, m).wait_recv()
            spread(pick, tok_all, tok_rows, j)
            if j == 0:

                @pl.loop(0, PEERS)
                def _(k):
                    plane(0, k).start()

            elif j == 1:

                @pl.loop(PEERS, WINDOW)
                def _(k):
                    plane(0, k).start()

                go_on(0, WINDOW, 2 * PEERS)
            else:
                go_on(0, j * PEERS, j * PEERS + (PEERS if j < DP - 1 else PEERS // 2))
        if m == 2:
            for n in range(1, SIDE):
                gathers[1][n].wait_recv()
                forward(1, n).start()
            for copy in columns:
                copy.start()
    own_rows[0].start()
    gathers[1][0].wait_recv()
    own[1].wait()
    for n in range(1, SIDE):
        forward(1, n).wait_recv()

    @pl.loop(0, DP)
    def _(j):
        spread(weight, grd_all, grd_rows, j)

    own_rows[1].start()
    go_on(0, SENDS - PEERS + PEERS // 2, SENDS)

    @pl.loop(0, WINDOW)
    def _(k):
        plane(0, SENDS - WINDOW + k).wait_send()
        plane(1, k).start()

    go_on(1, WINDOW, SENDS)

    @pl.loop(SENDS - WINDOW, SENDS)
    def _(k):
        plane(1, k).wait_send()

    for i in range(2):

        @pl.loop(0, SENDS)
        def _(k):
            plane(i, k).wait_recv()

    for i in range(2):
        for copy in gathers[i]:
            copy.wait_send()
        for m in range(1, SIDE):
            forward(i, m).wait_send()
    for copy in columns + own_rows:
        copy.wait()


def exchange(tokens, grd, pick, weight, p, q, r):
    tok, width = grd.shape
    dma = pltpu.SemaphoreType.DMA
    rows = (EP, DP, CAP, width)
    return pl.pallas_call(
        exchange_kernel,
        out_shape=[jax.ShapeDtypeStruct(rows, BF16)] * 2 + [jax.ShapeDtypeStruct(p.shape, BF16)] * 3,
        in_specs=[ANY, ANY, VMEM, VMEM, ANY, ANY, ANY],
        out_specs=[ANY] * 5,
        scratch_shapes=[
            pltpu.VMEM((DP, tok, width), BF16),
            pltpu.VMEM((DP, tok, width), BF16),
            pltpu.VMEM(rows, BF16),
            pltpu.VMEM(rows, BF16),
            dma((2, SENDS)), dma((2, SENDS)), dma((3, DP - 1)), dma((3, DP - 1)),
            dma((2, SIDE)), dma((2, SIDE)), dma((2, SIDE - 1)), dma((2, SIDE - 1)), dma((7,)),
        ],
        compiler_params=pltpu.CompilerParams(
            collective_id=1, has_side_effects=True, vmem_limit_bytes=63 * 2**20
        ),
        name="exchange",
    )(tokens, grd, pick, weight, p, q, r)


NT = (((1,), (1,)), ((), ()))
TN = (((0,), (0,)), ((), ()))


def dot(a, b, dims=(((1,), (0,)), ((), ()))):
    return lax.dot_general(a, b, dims, preferred_element_type=F32)


ORDER_Y = sum((step // SIDE) << (2 * n) for n, step in enumerate(PLANE_STEPS))
ORDER_X = sum((step % SIDE) << (2 * n) for n, step in enumerate(PLANE_STEPS))
ORDER_COLUMN = sum(step << (3 * n) for n, step in enumerate(COLUMN_STEPS))
GROUP = 2
ROWS = DP * CAP
SLAB = 256


def ordered_plane(n):
    me = lax.axis_index("expert")
    y, x = me // SIDE, me % SIDE
    dy, dx = (ORDER_Y >> (2 * n)) & 3, (ORDER_X >> (2 * n)) & 3
    ahead = ((y + dy) % SIDE) * SIDE + (x + dx) % SIDE
    behind = ((y + SIDE - dy) % SIDE) * SIDE + (x + SIDE - dx) % SIDE
    return ahead, behind


def ordered_column(n):
    me = lax.axis_index("dp")
    z, core = me // 2, me % 2
    step = (ORDER_COLUMN >> (3 * n)) & 7
    dz, other = step // 2, (core + step % 2) % 2
    return ((z + dz) % SIDE) * 2 + other, ((z + SIDE - dz) % SIDE) * 2 + other


def expert_kernel(
    x, u, wg, wu, wd, weight, pick, mixed, tokens_grad, out_back, rg_back, dg, du, dd,
    wgv, wuv, wdv, hid, gg, ug, rows_in, slabs, out_v, rg_v, paired, arrived,
    psend, precv, csend, crecv, wload, rload, sload, own, bload, xsend, xrecv, zsend, zrecv,
):
    dp, ep = lax.axis_index("dp"), lax.axis_index("expert")
    z, core = dp // 2, dp % 2
    weights = [
        pltpu.make_async_copy(src, dst, wload.at[i])
        for i, (src, dst) in enumerate(((wg, wgv), (wu, wuv), (wd, wdv)))
    ]
    backs = ((out_v, out_back), (rg_v, rg_back))

    def ahead(n):
        return (0b00110110 >> (2 * n)) & 3

    def row_loads(n, slot):
        loads = []
        for part in range(GROUP):
            source = ordered_plane(n * GROUP + part)[0]
            for i, src in enumerate((x, u)):
                loads.append(pltpu.make_async_copy(
                    src.at[source], rows_in.at[i, slot, pl.ds(part * DP, DP)], rload.at[i, slot, part]
                ))
        return loads

    def slab_loads(n, slot):
        column = pl.multiple_of(ordered_column(n)[0] * SLAB, SLAB)
        return [
            pltpu.make_async_copy(src.at[:, :, :, pl.ds(column, SLAB)], slabs.at[i, slot], sload.at[i, slot])
            for i, src in enumerate((x, u))
        ]

    def back(i, k):
        src, dst = backs[i]
        n, part = (k // DP, k % DP) if i == 0 else (k % PEERS, k // PEERS)
        target = ordered_plane(n)[0]
        part = (z + ahead(part // 2)) % SIDE * 2 + part % 2
        return pltpu.make_async_remote_copy(
            src_ref=src.at[target, part], dst_ref=dst.at[ep, part],
            send_sem=psend.at[i, k], recv_sem=precv.at[i, k],
            device_id=(dp, target), device_id_type=MESH,
        )

    def own_back(i):
        return pltpu.make_async_copy(backs[i][0].at[ep], backs[i][1].at[ep], own.at[i])

    slices = ((wgv, dg), (wuv, du), (wdv, dd))

    def grads(n):
        target = ordered_column(n)[0]
        part = pl.ds(pl.multiple_of(target * SLAB, SLAB), SLAB)
        return [
            pltpu.make_async_remote_copy(
                src_ref=src.at[part], dst_ref=dst.at[dp],
                send_sem=csend.at[i, n], recv_sem=crecv.at[i, n],
                device_id=(target, ep), device_id_type=MESH,
            )
            for i, (src, dst) in enumerate(slices)
        ]

    def own_grads():
        part = pl.ds(pl.multiple_of(dp * SLAB, SLAB), SLAB)
        return [
            pltpu.make_async_copy(src.at[part], dst.at[dp], own.at[2 + i])
            for i, (src, dst) in enumerate(slices)
        ]

    def back_load(i, source, slot):
        return pltpu.make_async_copy(backs[i][1].at[:, source], rows_in.at[0, slot], bload.at[slot])

    def pair_copy(i, n):
        place = ((z + ahead(n)) % SIDE) * 2 + 1 - core
        return to_column(1, out_v.at[place], paired.at[i, n], xsend.at[i, n], xrecv.at[i, n])

    def z_copy(i, n):
        place = ((z + ahead(n)) % SIDE) * 2 + core
        return to_column(2 * ahead(n), out_v.at[place], arrived.at[i, n], zsend.at[i, n], zrecv.at[i, n])

    def collect(i, matrix, n):
        chip = (z + ahead(n)) % SIDE
        places = (chip * 2 + 1 - core, chip * 2 + core)
        for slot in range(2):
            back_load(i, places[slot], slot).start()
        for slot in range(2):
            back_load(i, places[slot], slot).wait()
            held = rows_in[0, slot]
            summed = dot(matrix[places[slot]], held.reshape(EP * CAP, held.shape[-1]), TN).astype(BF16)
            out_v[places[slot]] = summed.reshape(out_v.shape[1:])
            if slot == 0:
                pair_copy(i, n).start()

    def add_pair(i, n):
        place = ((z + ahead(n)) % SIDE) * 2 + core
        pair_copy(i, n).wait_recv()
        out_v[place] = (out_v[place].astype(F32) + paired[i, n].astype(F32)).astype(BF16)
        if n < SIDE - 1:
            z_copy(i, n).start()

    def finish(i, result):
        total = out_v[dp].astype(F32)
        for n in range(SIDE - 1):
            z_copy(i, n).wait_recv()
            total += arrived[i, n].astype(F32)
        result[...] = total.astype(BF16).reshape(result.shape)
        for n in range(SIDE):
            pair_copy(i, n).wait_send()
        for n in range(SIDE - 1):
            z_copy(i, n).wait_send()

    for copy in weights + row_loads(0, 0):
        copy.start()
    greet(COLUMN_STEPS, PLANE_STEPS)
    for copy in weights:
        copy.wait()

    groups = EP // GROUP

    @pl.loop(0, groups)
    def _(n):
        slot = n % 2
        for copy in row_loads(n, slot):
            copy.wait()

        @pl.when(n + 1 < groups)
        def _():
            for copy in row_loads(n + 1, 1 - slot):
                copy.start()

        shape = (GROUP * ROWS, rows_in.shape[-1])
        xb, ub = rows_in[0, slot].reshape(shape), rows_in[1, slot].reshape(shape)
        gate, up = dot(xb, wgv[...]), dot(xb, wuv[...])
        s = jax.nn.sigmoid(gate)
        hidden = (gate * s * up).astype(BF16)
        out = dot(hidden, wdv[...], NT).astype(BF16)
        hg = dot(ub, wdv[...])
        gate_grad = (hg * up * s * (1.0 + gate * (1.0 - s))).astype(BF16)
        up_grad = (hg * gate * s).astype(BF16)
        rg = (dot(gate_grad, wgv[...], NT) + dot(up_grad, wuv[...], NT)).astype(BF16)
        for part in range(GROUP):
            source = ordered_plane(n * GROUP + part)[0]
            these = slice(part * ROWS, (part + 1) * ROWS)
            out_v[source] = out[these].reshape(DP, CAP, -1)
            rg_v[source] = rg[these].reshape(DP, CAP, -1)
            held = pl.ds(pl.multiple_of(source * ROWS, ROWS), ROWS)
            hid[held], gg[held], ug[held] = hidden[these], gate_grad[these], up_grad[these]
        @pl.loop(0, 10)
        def _(j):
            back(0, n * 10 + j).start()

    first = 10 * groups

    for i in range(2):
        own_back(i).start()
    for copy in slab_loads(0, 0):
        copy.start()

    @pl.loop(0, DP)
    def _(n):
        slot = n % 2
        for copy in slab_loads(n, slot):
            copy.wait()

        @pl.when(n + 1 < DP)
        def _():
            for copy in slab_loads(n + 1, 1 - slot):
                copy.start()

        part = pl.ds(pl.multiple_of(ordered_column(n)[0] * SLAB, SLAB), SLAB)
        shape = (EP * ROWS, SLAB)
        wgv[part] = dot(slabs[0, slot].reshape(shape), gg[...], TN).astype(BF16)
        wuv[part] = dot(slabs[0, slot].reshape(shape), ug[...], TN).astype(BF16)
        wdv[part] = dot(slabs[1, slot].reshape(shape), hid[...], TN).astype(BF16)

        @pl.when(n + 1 < DP)
        def _():
            for copy in grads(n):
                copy.start()

        @pl.when(n + 1 == DP)
        def _():
            for copy in own_grads():
                copy.start()

        @pl.loop(0, (SENDS - first) // DP)
        def _(j):
            k = first + n * ((SENDS - first) // DP) + j
            back(0, k - WINDOW).wait_send()
            back(0, k).start()

    @pl.loop(0, WINDOW)
    def _(k):
        back(0, SENDS - WINDOW + k).wait_send()
        back(1, k).start()

    def go_on(start, stop):
        @pl.loop(start, stop)
        def _(k):
            back(1, k - WINDOW).wait_send()
            back(1, k).start()

    go_on(WINDOW, 56)

    @pl.loop(0, first - WINDOW)
    def _(k):
        back(0, k).wait_send()

    @pl.loop(0, SENDS)
    def _(k):
        back(0, k).wait_recv()

    own_back(0).wait()
    for n in range(SIDE):
        collect(0, weight, n)
    go_on(56, 80)
    for n in range(SIDE):
        add_pair(0, n)
    go_on(80, 104)
    finish(0, mixed)
    go_on(104, SENDS)
    own_back(1).wait()
    for n in range(SIDE):

        @pl.loop(n * 2 * PEERS, (n + 1) * 2 * PEERS)
        def _(k):
            back(1, k).wait_recv()

        collect(1, pick, n)
        if n > 0:
            add_pair(1, n - 1)
    add_pair(1, SIDE - 1)
    finish(1, tokens_grad)

    @pl.loop(SENDS - WINDOW, SENDS)
    def _(k):
        back(1, k).wait_send()

    for copy in own_grads():
        copy.wait()

    @pl.loop(0, DP - 1)
    def _(n):
        for copy in grads(n):
            copy.wait()


def expert(x, u, wg, wu, wd, weight, pick):
    width = x.shape[-1]
    ff = wg.shape[1]
    tok = weight.shape[-1]
    dma = pltpu.SemaphoreType.DMA
    block = (DP, CAP, width)
    results = pl.pallas_call(
        expert_kernel,
        out_shape=[jax.ShapeDtypeStruct((tok, width), BF16)] * 2
        + [jax.ShapeDtypeStruct((EP, DP, CAP, width), BF16)] * 2
        + [jax.ShapeDtypeStruct((DP, width // DP, ff), BF16)] * 3,
        in_specs=[ANY] * 5 + [VMEM] * 2,
        out_specs=[VMEM] * 2 + [ANY] * 5,
        scratch_shapes=[pltpu.VMEM((width, ff), BF16)] * 3
        + [pltpu.VMEM((EP * ROWS, ff), BF16)] * 3
        + [
            pltpu.VMEM((2, 2, GROUP * DP, CAP, width), BF16),
            pltpu.VMEM((2, 2, EP, DP, CAP, SLAB), BF16),
            pltpu.VMEM((EP,) + block, BF16),
            pltpu.VMEM((EP,) + block, BF16),
            pltpu.VMEM((2, SIDE) + block, BF16),
            pltpu.VMEM((2, SIDE - 1) + block, BF16),
            dma((2, SENDS)), dma((2, SENDS)), dma((3, DP - 1)), dma((3, DP - 1)),
            dma((3,)), dma((2, 2, GROUP)), dma((2, 2)), dma((5,)), dma((2,)),
            dma((2, SIDE)), dma((2, SIDE)), dma((2, SIDE - 1)), dma((2, SIDE - 1)),
        ],
        compiler_params=pltpu.CompilerParams(
            collective_id=2, has_side_effects=True, vmem_limit_bytes=63 * 2**20
        ),
        name="expert",
    )(x, u, wg, wu, wd, weight, pick)
    return results[0], results[1], *results[4:]


def local(tokens, expert_ids, gate_codes, grad_out, w_gate, w_up, w_down):
    dp = lax.axis_index("dp")
    tok, width = tokens.shape
    ff = w_gate.shape[-1]
    meta = (expert_ids * 256 + gate_codes).T
    meta_all = gather_column(meta)
    ids, codes = meta_all // 256, meta_all % 256
    mine = jnp.arange(EP, dtype=jnp.int32) * DP + dp
    named = ids[:, None] == mine[None, :, None, None]
    has = jnp.any(named, axis=2)
    gate = jnp.sum(jnp.where(named, codes[:, None], 0), axis=2).astype(F32) / 256.0
    earlier = jnp.triu(jnp.ones((tok, tok), BF16), 1)
    rank = jnp.dot(has.astype(BF16), earlier, preferred_element_type=F32).astype(jnp.int32)
    slot = jnp.where(has, rank, -1)[:, :, None, :]
    pick = slot == jnp.arange(CAP, dtype=jnp.int32)[None, None, :, None]
    weight = jnp.where(pick, gate[:, :, None, :], 0.0).astype(BF16).reshape(DP, EP * CAP, tok)
    pick = pick.astype(BF16).reshape(DP, EP * CAP, tok)
    x, u, wg, wu, wd = exchange(tokens, grad_out, pick, weight, w_gate, w_up, w_down)
    wg, wu, wd = (w.reshape(width, ff) for w in (wg, wu, wd))
    return expert(x, u, wg, wu, wd, weight, pick)


def solution(mesh):
    rows, weights = P(("dp", "expert"), None), P("expert", "dp", None)
    return jax.shard_map(
        local,
        mesh=mesh,
        in_specs=(rows,) * 4 + (weights,) * 3,
        out_specs=(rows,) * 2 + (weights,) * 3,
        check_vma=False,
    )
```

```python
import jax
import jax.numpy as jnp
from jax import lax
from jax.experimental import pallas as pl
from jax.experimental.pallas import tpu as pltpu
from jax.sharding import PartitionSpec as P

BF16 = jnp.bfloat16
F32 = jnp.float32
MESH = pl.DeviceIdType.MESH
ANY = pl.BlockSpec(memory_space=pl.ANY)
VMEM = pl.BlockSpec(memory_space=pltpu.VMEM)
DP = 8
EP = 16
SIDE = 4
CAP = 16
TOK = 128


def column_peer(step):
    me = lax.axis_index("dp")
    z, core = me // 2, me % 2
    dz, other = step // 2, (core + step % 2) % 2
    return ((z + dz) % SIDE) * 2 + other, ((z + SIDE - dz) % SIDE) * 2 + other


def plane_peer(step):
    me = lax.axis_index("expert")
    y, x = me // SIDE, me % SIDE
    dy, dx = step // SIDE, step % SIDE
    ahead = ((y + dy) % SIDE) * SIDE + (x + dx) % SIDE
    behind = ((y + SIDE - dy) % SIDE) * SIDE + (x + SIDE - dx) % SIDE
    return ahead, behind


PLANE_STEPS = (1, 3, 4, 12, 5, 15, 7, 13, 10, 2, 8, 6, 14, 9, 11)
COLUMN_STEPS = (4, 5, 2, 3, 6, 7, 1)


def greet(column, plane):
    barrier = pltpu.get_barrier_semaphore()
    dp, ep = lax.axis_index("dp"), lax.axis_index("expert")
    count = 0
    for step in column:
        pl.semaphore_signal(barrier, inc=1, device_id=(column_peer(step)[0], ep), device_id_type=MESH)
        count += 1
    for step in plane:
        pl.semaphore_signal(barrier, inc=1, device_id=(dp, plane_peer(step)[0]), device_id_type=MESH)
        count += 1
    pl.semaphore_wait(barrier, count)


def to_column(step, src, dst, send, recv):
    return pltpu.make_async_remote_copy(
        src_ref=src, dst_ref=dst, send_sem=send, recv_sem=recv,
        device_id=(column_peer(step)[0], lax.axis_index("expert")), device_id_type=MESH,
    )


def to_plane(step, src, dst, send, recv):
    return pltpu.make_async_remote_copy(
        src_ref=src, dst_ref=dst, send_sem=send, recv_sem=recv,
        device_id=(lax.axis_index("dp"), plane_peer(step)[0]), device_id_type=MESH,
    )


def gather_kernel(meta, meta_all, send, recv, local):
    me = lax.axis_index("dp")
    greet(COLUMN_STEPS, ())
    copies = [
        to_column(step, meta, meta_all.at[me], send.at[n], recv.at[n]) for n, step in enumerate(COLUMN_STEPS)
    ]
    copies.append(pltpu.make_async_copy(meta, meta_all.at[me], local))
    for copy in copies:
        copy.start()
    for copy in copies:
        copy.wait()


def gather_column(meta):
    dma = pltpu.SemaphoreType.DMA
    return pl.pallas_call(
        gather_kernel,
        out_shape=jax.ShapeDtypeStruct((DP,) + meta.shape, meta.dtype),
        in_specs=[ANY],
        out_specs=ANY,
        scratch_shapes=[dma((DP - 1,)), dma((DP - 1,)), dma],
        compiler_params=pltpu.CompilerParams(collective_id=0, has_side_effects=True),
        name="gather_column",
    )(meta)


PEERS = EP - 1
SENDS = DP * PEERS
WINDOW = 24


def exchange_kernel(tok, grd, pick, weight, p, q, r, a_out, b_out, p_out, q_out, r_out,
                    tok_all, grd_all, tok_rows, grd_rows,
                    psend, precv, csend, crecv, gsend, grecv, fsend, frecv, local):
    dp, ep = lax.axis_index("dp"), lax.axis_index("expert")
    z, core = dp // 2, dp % 2
    gathered = ((tok, tok_all), (grd, grd_all))

    def place(j):
        return (z + ((0b10110100 >> (j // 2 * 2)) & 3)) % SIDE * 2 + (core + j % 2) % 2

    own = [
        pltpu.make_async_copy(src, dst.at[dp], local.at[5 + i]) for i, (src, dst) in enumerate(gathered)
    ]
    own[0].start()
    greet(COLUMN_STEPS, PLANE_STEPS)
    gathers = [
        [
            to_column(step, src, dst.at[dp], gsend.at[i, n], grecv.at[i, n])
            for n, step in enumerate((1, 6, 2, 4))
        ]
        for i, (src, dst) in enumerate(gathered)
    ]

    def forward(i, m):
        block = gathered[i][1].at[place(2 * m)]
        return to_column(1, block, block, fsend.at[i, m - 1], frecv.at[i, m - 1])

    columns = []
    for n, step in enumerate(COLUMN_STEPS):
        target = column_peer(step)[0]
        for i, (src, dst) in enumerate(((p, p_out), (q, q_out), (r, r_out))):
            columns.append(to_column(step, src.at[target], dst.at[dp], csend.at[i, n], crecv.at[i, n]))
    for i, (src, dst) in enumerate(((p, p_out), (q, q_out), (r, r_out))):
        columns.append(pltpu.make_async_copy(src.at[dp], dst.at[dp], local.at[i]))
    own_rows = [
        pltpu.make_async_copy(src.at[ep], dst.at[ep], local.at[3 + i])
        for i, (src, dst) in enumerate(((tok_rows, a_out), (grd_rows, b_out)))
    ]
    ends = ((tok_rows, a_out), (grd_rows, b_out))

    def plane(i, k):
        src, dst = ends[i]
        target, part = ordered_plane(k % PEERS)[0], place(k // PEERS)
        return pltpu.make_async_remote_copy(
            src_ref=src.at[target, part], dst_ref=dst.at[ep, part],
            send_sem=psend.at[i, k], recv_sem=precv.at[i, k],
            device_id=(dp, target), device_id_type=MESH,
        )

    def go_on(i, start, stop):
        @pl.loop(start, stop)
        def _(k):
            plane(i, k - WINDOW).wait_send()
            plane(i, k).start()

    def spread(matrix, rows, result, j):
        part = place(j)
        picked = dot(matrix[part], rows[part]).astype(BF16)
        result[:, part] = picked.reshape(EP, CAP, picked.shape[-1])

    for copy in gathers[0] + gathers[1] + own[1:]:
        copy.start()
    own[0].wait()
    for m in range(SIDE):
        if m:
            gathers[0][m].wait_recv()
            forward(0, m).start()
        for j in (2 * m, 2 * m + 1):
            if j == 1:
                gathers[0][0].wait_recv()
            elif j % 2:
                forward(0, m).wait_recv()
            spread(pick, tok_all, tok_rows, j)
            if j == 0:

                @pl.loop(0, PEERS)
                def _(k):
                    plane(0, k).start()

            elif j == 1:

                @pl.loop(PEERS, WINDOW)
                def _(k):
                    plane(0, k).start()

                go_on(0, WINDOW, 2 * PEERS)
            else:
                go_on(0, j * PEERS, j * PEERS + (PEERS if j < DP - 1 else PEERS // 2))
        if m == 2:
            for n in range(1, SIDE):
                gathers[1][n].wait_recv()
                forward(1, n).start()
            for copy in columns:
                copy.start()
    own_rows[0].start()
    gathers[1][0].wait_recv()
    own[1].wait()
    for n in range(1, SIDE):
        forward(1, n).wait_recv()

    @pl.loop(0, DP)
    def _(j):
        spread(weight, grd_all, grd_rows, j)

    own_rows[1].start()
    go_on(0, SENDS - PEERS + PEERS // 2, SENDS)

    @pl.loop(0, WINDOW)
    def _(k):
        plane(0, SENDS - WINDOW + k).wait_send()
        plane(1, k).start()

    go_on(1, WINDOW, SENDS)

    @pl.loop(SENDS - WINDOW, SENDS)
    def _(k):
        plane(1, k).wait_send()

    for i in range(2):

        @pl.loop(0, SENDS)
        def _(k):
            plane(i, k).wait_recv()

    for i in range(2):
        for copy in gathers[i]:
            copy.wait_send()
        for m in range(1, SIDE):
            forward(i, m).wait_send()
    for copy in columns + own_rows:
        copy.wait()


def exchange(tokens, grd, pick, weight, p, q, r):
    tok, width = grd.shape
    dma = pltpu.SemaphoreType.DMA
    rows = (EP, DP, CAP, width)
    return pl.pallas_call(
        exchange_kernel,
        out_shape=[jax.ShapeDtypeStruct(rows, BF16)] * 2 + [jax.ShapeDtypeStruct(p.shape, BF16)] * 3,
        in_specs=[ANY, ANY, VMEM, VMEM, ANY, ANY, ANY],
        out_specs=[ANY] * 5,
        scratch_shapes=[
            pltpu.VMEM((DP, tok, width), BF16),
            pltpu.VMEM((DP, tok, width), BF16),
            pltpu.VMEM(rows, BF16),
            pltpu.VMEM(rows, BF16),
            dma((2, SENDS)), dma((2, SENDS)), dma((3, DP - 1)), dma((3, DP - 1)),
            dma((2, SIDE)), dma((2, SIDE)), dma((2, SIDE - 1)), dma((2, SIDE - 1)), dma((7,)),
        ],
        compiler_params=pltpu.CompilerParams(
            collective_id=1, has_side_effects=True, vmem_limit_bytes=63 * 2**20
        ),
        name="exchange",
    )(tokens, grd, pick, weight, p, q, r)


NT = (((1,), (1,)), ((), ()))
TN = (((0,), (0,)), ((), ()))


def dot(a, b, dims=(((1,), (0,)), ((), ()))):
    return lax.dot_general(a, b, dims, preferred_element_type=F32)


ORDER_Y = sum((step // SIDE) << (2 * n) for n, step in enumerate(PLANE_STEPS))
ORDER_X = sum((step % SIDE) << (2 * n) for n, step in enumerate(PLANE_STEPS))
ORDER_COLUMN = sum(step << (3 * n) for n, step in enumerate(COLUMN_STEPS))
GROUP = 2
ROWS = DP * CAP
SLAB = 256


def ordered_plane(n):
    me = lax.axis_index("expert")
    y, x = me // SIDE, me % SIDE
    dy, dx = (ORDER_Y >> (2 * n)) & 3, (ORDER_X >> (2 * n)) & 3
    ahead = ((y + dy) % SIDE) * SIDE + (x + dx) % SIDE
    behind = ((y + SIDE - dy) % SIDE) * SIDE + (x + SIDE - dx) % SIDE
    return ahead, behind


def ordered_column(n):
    me = lax.axis_index("dp")
    z, core = me // 2, me % 2
    step = (ORDER_COLUMN >> (3 * n)) & 7
    dz, other = step // 2, (core + step % 2) % 2
    return ((z + dz) % SIDE) * 2 + other, ((z + SIDE - dz) % SIDE) * 2 + other


def expert_kernel(
    x, u, wg, wu, wd, weight, pick, mixed, tokens_grad, out_back, rg_back, dg, du, dd,
    wgv, wuv, wdv, hid, gg, ug, rows_in, slabs, out_v, rg_v, paired, arrived,
    psend, precv, csend, crecv, wload, rload, sload, own, bload, xsend, xrecv, zsend, zrecv,
):
    dp, ep = lax.axis_index("dp"), lax.axis_index("expert")
    z, core = dp // 2, dp % 2
    weights = [
        pltpu.make_async_copy(src, dst, wload.at[i])
        for i, (src, dst) in enumerate(((wg, wgv), (wu, wuv), (wd, wdv)))
    ]
    backs = ((out_v, out_back), (rg_v, rg_back))

    def ahead(n):
        return (0b00110110 >> (2 * n)) & 3

    def row_loads(n, slot):
        loads = []
        for part in range(GROUP):
            source = ordered_plane(n * GROUP + part)[0]
            for i, src in enumerate((x, u)):
                loads.append(pltpu.make_async_copy(
                    src.at[source], rows_in.at[i, slot, pl.ds(part * DP, DP)], rload.at[i, slot, part]
                ))
        return loads

    def slab_loads(n, slot):
        column = pl.multiple_of(ordered_column(n)[0] * SLAB, SLAB)
        return [
            pltpu.make_async_copy(src.at[:, :, :, pl.ds(column, SLAB)], slabs.at[i, slot], sload.at[i, slot])
            for i, src in enumerate((x, u))
        ]

    def back(i, k):
        src, dst = backs[i]
        n, part = (k // DP, k % DP) if i == 0 else (k % PEERS, k // PEERS)
        target = ordered_plane(n)[0]
        part = (z + ahead(part // 2)) % SIDE * 2 + part % 2
        return pltpu.make_async_remote_copy(
            src_ref=src.at[target, part], dst_ref=dst.at[ep, part],
            send_sem=psend.at[i, k], recv_sem=precv.at[i, k],
            device_id=(dp, target), device_id_type=MESH,
        )

    def own_back(i):
        return pltpu.make_async_copy(backs[i][0].at[ep], backs[i][1].at[ep], own.at[i])

    slices = ((wgv, dg), (wuv, du), (wdv, dd))

    def grads(n):
        target = ordered_column(n)[0]
        part = pl.ds(pl.multiple_of(target * SLAB, SLAB), SLAB)
        return [
            pltpu.make_async_remote_copy(
                src_ref=src.at[part], dst_ref=dst.at[dp],
                send_sem=csend.at[i, n], recv_sem=crecv.at[i, n],
                device_id=(target, ep), device_id_type=MESH,
            )
            for i, (src, dst) in enumerate(slices)
        ]

    def own_grads():
        part = pl.ds(pl.multiple_of(dp * SLAB, SLAB), SLAB)
        return [
            pltpu.make_async_copy(src.at[part], dst.at[dp], own.at[2 + i])
            for i, (src, dst) in enumerate(slices)
        ]

    def back_load(i, source, slot):
        return pltpu.make_async_copy(backs[i][1].at[:, source], rows_in.at[0, slot], bload.at[slot])

    def pair_copy(i, n):
        place = ((z + ahead(n)) % SIDE) * 2 + 1 - core
        return to_column(1, out_v.at[place], paired.at[i, n], xsend.at[i, n], xrecv.at[i, n])

    def z_copy(i, n):
        place = ((z + ahead(n)) % SIDE) * 2 + core
        return to_column(2 * ahead(n), out_v.at[place], arrived.at[i, n], zsend.at[i, n], zrecv.at[i, n])

    def collect(i, matrix, n):
        chip = (z + ahead(n)) % SIDE
        places = (chip * 2 + 1 - core, chip * 2 + core)
        for slot in range(2):
            back_load(i, places[slot], slot).start()
        for slot in range(2):
            back_load(i, places[slot], slot).wait()
            held = rows_in[0, slot]
            summed = dot(matrix[places[slot]], held.reshape(EP * CAP, held.shape[-1]), TN).astype(BF16)
            out_v[places[slot]] = summed.reshape(out_v.shape[1:])
            if slot == 0:
                pair_copy(i, n).start()

    def add_pair(i, n):
        place = ((z + ahead(n)) % SIDE) * 2 + core
        pair_copy(i, n).wait_recv()
        out_v[place] = (out_v[place].astype(F32) + paired[i, n].astype(F32)).astype(BF16)
        if n < SIDE - 1:
            z_copy(i, n).start()

    def finish(i, result):
        total = out_v[dp].astype(F32)
        for n in range(SIDE - 1):
            z_copy(i, n).wait_recv()
            total += arrived[i, n].astype(F32)
        result[...] = total.astype(BF16).reshape(result.shape)
        for n in range(SIDE):
            pair_copy(i, n).wait_send()
        for n in range(SIDE - 1):
            z_copy(i, n).wait_send()

    for copy in weights + row_loads(0, 0):
        copy.start()
    greet(COLUMN_STEPS, PLANE_STEPS)
    for copy in weights:
        copy.wait()

    groups = EP // GROUP

    @pl.loop(0, groups)
    def _(n):
        slot = n % 2
        for copy in row_loads(n, slot):
            copy.wait()

        @pl.when(n + 1 < groups)
        def _():
            for copy in row_loads(n + 1, 1 - slot):
                copy.start()

        shape = (GROUP * ROWS, rows_in.shape[-1])
        xb, ub = rows_in[0, slot].reshape(shape), rows_in[1, slot].reshape(shape)
        gate, up = dot(xb, wgv[...]), dot(xb, wuv[...])
        s = jax.nn.sigmoid(gate)
        hidden = (gate * s * up).astype(BF16)
        out = dot(hidden, wdv[...], NT).astype(BF16)
        hg = dot(ub, wdv[...])
        gate_grad = (hg * up * s * (1.0 + gate * (1.0 - s))).astype(BF16)
        up_grad = (hg * gate * s).astype(BF16)
        rg = (dot(gate_grad, wgv[...], NT) + dot(up_grad, wuv[...], NT)).astype(BF16)
        for part in range(GROUP):
            source = ordered_plane(n * GROUP + part)[0]
            these = slice(part * ROWS, (part + 1) * ROWS)
            out_v[source] = out[these].reshape(DP, CAP, -1)
            rg_v[source] = rg[these].reshape(DP, CAP, -1)
            held = pl.ds(pl.multiple_of(source * ROWS, ROWS), ROWS)
            hid[held], gg[held], ug[held] = hidden[these], gate_grad[these], up_grad[these]
        @pl.loop(0, 12)
        def _(j):
            back(0, n * 12 + j).start()

    first = 12 * groups

    for i in range(2):
        own_back(i).start()
    for copy in slab_loads(0, 0):
        copy.start()

    @pl.loop(0, DP)
    def _(n):
        slot = n % 2
        for copy in slab_loads(n, slot):
            copy.wait()

        @pl.when(n + 1 < DP)
        def _():
            for copy in slab_loads(n + 1, 1 - slot):
                copy.start()

        part = pl.ds(pl.multiple_of(ordered_column(n)[0] * SLAB, SLAB), SLAB)
        shape = (EP * ROWS, SLAB)
        wgv[part] = dot(slabs[0, slot].reshape(shape), gg[...], TN).astype(BF16)
        wuv[part] = dot(slabs[0, slot].reshape(shape), ug[...], TN).astype(BF16)
        wdv[part] = dot(slabs[1, slot].reshape(shape), hid[...], TN).astype(BF16)

        @pl.when(n + 1 < DP)
        def _():
            for copy in grads(n):
                copy.start()

        @pl.when(n + 1 == DP)
        def _():
            for copy in own_grads():
                copy.start()

        @pl.when(n < (SENDS - first) // 4)
        def _():
            for j in range(4):
                back(0, first - WINDOW + 4 * n + j).wait_send()
                back(0, first + 4 * n + j).start()

    @pl.loop(0, WINDOW)
    def _(k):
        back(0, SENDS - WINDOW + k).wait_send()
        back(1, k).start()

    def go_on(start, stop):
        @pl.loop(start, stop)
        def _(k):
            back(1, k - WINDOW).wait_send()
            back(1, k).start()

    go_on(WINDOW, 56)

    @pl.loop(0, first - WINDOW)
    def _(k):
        back(0, k).wait_send()

    @pl.loop(0, SENDS)
    def _(k):
        back(0, k).wait_recv()

    own_back(0).wait()
    for n in range(SIDE):
        collect(0, weight, n)
    go_on(56, 80)
    for n in range(SIDE):
        add_pair(0, n)
    go_on(80, 104)
    finish(0, mixed)
    go_on(104, SENDS)
    own_back(1).wait()
    for n in range(SIDE):

        @pl.loop(n * 2 * PEERS, (n + 1) * 2 * PEERS)
        def _(k):
            back(1, k).wait_recv()

        collect(1, pick, n)
        if n > 0:
            add_pair(1, n - 1)
    add_pair(1, SIDE - 1)
    finish(1, tokens_grad)

    @pl.loop(SENDS - WINDOW, SENDS)
    def _(k):
        back(1, k).wait_send()

    for copy in own_grads():
        copy.wait()

    @pl.loop(0, DP - 1)
    def _(n):
        for copy in grads(n):
            copy.wait()


def expert(x, u, wg, wu, wd, weight, pick):
    width = x.shape[-1]
    ff = wg.shape[1]
    tok = weight.shape[-1]
    dma = pltpu.SemaphoreType.DMA
    block = (DP, CAP, width)
    results = pl.pallas_call(
        expert_kernel,
        out_shape=[jax.ShapeDtypeStruct((tok, width), BF16)] * 2
        + [jax.ShapeDtypeStruct((EP, DP, CAP, width), BF16)] * 2
        + [jax.ShapeDtypeStruct((DP, width // DP, ff), BF16)] * 3,
        in_specs=[ANY] * 5 + [VMEM] * 2,
        out_specs=[VMEM] * 2 + [ANY] * 5,
        scratch_shapes=[pltpu.VMEM((width, ff), BF16)] * 3
        + [pltpu.VMEM((EP * ROWS, ff), BF16)] * 3
        + [
            pltpu.VMEM((2, 2, GROUP * DP, CAP, width), BF16),
            pltpu.VMEM((2, 2, EP, DP, CAP, SLAB), BF16),
            pltpu.VMEM((EP,) + block, BF16),
            pltpu.VMEM((EP,) + block, BF16),
            pltpu.VMEM((2, SIDE) + block, BF16),
            pltpu.VMEM((2, SIDE - 1) + block, BF16),
            dma((2, SENDS)), dma((2, SENDS)), dma((3, DP - 1)), dma((3, DP - 1)),
            dma((3,)), dma((2, 2, GROUP)), dma((2, 2)), dma((5,)), dma((2,)),
            dma((2, SIDE)), dma((2, SIDE)), dma((2, SIDE - 1)), dma((2, SIDE - 1)),
        ],
        compiler_params=pltpu.CompilerParams(
            collective_id=2, has_side_effects=True, vmem_limit_bytes=63 * 2**20
        ),
        name="expert",
    )(x, u, wg, wu, wd, weight, pick)
    return results[0], results[1], *results[4:]


def local(tokens, expert_ids, gate_codes, grad_out, w_gate, w_up, w_down):
    dp = lax.axis_index("dp")
    tok, width = tokens.shape
    ff = w_gate.shape[-1]
    meta = (expert_ids * 256 + gate_codes).T
    meta_all = gather_column(meta)
    ids, codes = meta_all // 256, meta_all % 256
    mine = jnp.arange(EP, dtype=jnp.int32) * DP + dp
    named = ids[:, None] == mine[None, :, None, None]
    has = jnp.any(named, axis=2)
    gate = jnp.sum(jnp.where(named, codes[:, None], 0), axis=2).astype(F32) / 256.0
    earlier = jnp.triu(jnp.ones((tok, tok), BF16), 1)
    rank = jnp.dot(has.astype(BF16), earlier, preferred_element_type=F32).astype(jnp.int32)
    slot = jnp.where(has, rank, -1)[:, :, None, :]
    pick = slot == jnp.arange(CAP, dtype=jnp.int32)[None, None, :, None]
    weight = jnp.where(pick, gate[:, :, None, :], 0.0).astype(BF16).reshape(DP, EP * CAP, tok)
    pick = pick.astype(BF16).reshape(DP, EP * CAP, tok)
    x, u, wg, wu, wd = exchange(tokens, grad_out, pick, weight, w_gate, w_up, w_down)
    wg, wu, wd = (w.reshape(width, ff) for w in (wg, wu, wd))
    return expert(x, u, wg, wu, wd, weight, pick)


def solution(mesh):
    rows, weights = P(("dp", "expert"), None), P("expert", "dp", None)
    return jax.shard_map(
        local,
        mesh=mesh,
        in_specs=(rows,) * 4 + (weights,) * 3,
        out_specs=(rows,) * 2 + (weights,) * 3,
        check_vma=False,
    )
```
